32 devices in a mesh: wide: 8 (over y, x, core), blk: 4 (over z).
Axes of the slice: x: 2, y: 2, z: 4, core: 2. Of those that a mesh axis runs over, the one named last changes fastest.
Arguments:
- hidden: bfloat16 [4, 64, 8192], P('blk', 'wide'), may hold values from -400 to 400, as said below
- norm_gain: float32 [8192], replicated, may hold values from 0.1 to 1.9
- w_query: bfloat16 [8192, 8192], P('blk', 'wide'), may hold values from -0.0625 to 0.0625
- key_weight_matrix: bfloat16 [8192, 1024], P('blk'), may hold values from -0.0625 to 0.0625
- value_weight_matrix: bfloat16 [8192, 1024], P('blk'), may hold values from -0.0625 to 0.0625
- cache_key: bfloat16 [8192, 1024], P('blk'), may hold values from -90 to 90
- prefix_value_cache: bfloat16 [8192, 1024], P('blk'), may hold values from -5 to 5
- start: int32 [1], replicated, may hold values from 8192 to 130816
- reach: int32 [4, 64], P('blk'), may hold values from 0 to 8447
- passkey: int32 [16], replicated, may hold values from 0 to 8191
Outputs:
- attended: bfloat16 [4, 64, 8192], P('blk', 'wide')
The draws below stay inside these ranges and needn't reach their ends.
Inputs may be any that keep to these rules, and one draw needn't show every extreme that they name: hidden states of order one up to row and feature scales.
All inputs are finite; a program needn't handle non-finite values.
Results may differ from the reference program's by a relative error of at most 0.017.
The reference program's roundings to bfloat16 on the way (of `normed` and `weights`) count: a program that leaves them out, or rounds other values in their place, can miss the bound.
Values may be sent and summed in bfloat16 or wider, within the bound.
No kernel may reach another device: no remote copies, remote signals or barrier semaphores. Data moves between devices by JAX's collectives and lax.ppermute only.
A program may use at most 128 MiB of HBM per device.

```python
import math
import jax
import jax.numpy as jnp
from jax import lax

MODEL_WIDTH = 8192
QUERY_HEADS = 64
KEY_VALUE_HEADS = 8
HEAD_WIDTH = 128
CONTEXT = 131072
PREFIX_TOKENS = 8192
NPASS = 16
BT = 64
NB = 4
WINDOW = 256


def draw_hidden(key, part):
    first_operand, second_operand, third_operand = jax.random.split(key, 3)
    rotary_base = jnp.clip(jax.random.normal(first_operand, (NB, BT, MODEL_WIDTH), jnp.float32), -4.0, 4.0)
    rowscale = jnp.exp(jax.random.uniform(second_operand, (NB, BT, 1), jnp.float32, 0.0, math.log(10.0)))
    colscale = jnp.exp(jax.random.uniform(third_operand, (MODEL_WIDTH,), jnp.float32, 0.0, math.log(10.0)))
    return (rotary_base * rowscale * colscale[None, None, :]).astype(jnp.bfloat16)


def draw_cache_key(key, part):
    first_operand = jax.random.fold_in(key, 0)
    value_rows_all = jnp.clip(jax.random.normal(first_operand, (PREFIX_TOKENS, KEY_VALUE_HEADS * HEAD_WIDTH), jnp.float32), -4.0, 4.0)
    return value_rows_all.astype(jnp.bfloat16)


def plant(array, stream_key, least, high):
    shape = array.shape
    place = [jax.random.randint(jax.random.fold_in(stream_key, axis), (), 0, shape[axis]) for axis in range(len(shape))]
    array = array.at[tuple(place)].set(least)
    longest = shape.index(max(shape))
    place[longest] = (place[longest] + 1) % shape[longest]
    return array.at[tuple(place)].set(high)


def block_levels(rng, dims, cuts, low, top_value):
    loudness = 1.0
    for dim, parts in cuts:
        draws = jax.random.uniform(jax.random.fold_in(jax.random.fold_in(rng, 6), dim), (parts,), jnp.float32, low / len(cuts), top_value / len(cuts))
        loudness = loudness * jnp.repeat(jnp.exp(draws), dims[dim] // parts).reshape((-1,) + (1,) * (len(dims) - 1 - dim))
    return loudness


def bell_draw(own_key, extent, scale, bound, cuts=(), held_as=jnp.bfloat16):
    result = scale * jax.random.normal(own_key, extent, jnp.float32)
    if cuts:
        result = result * block_levels(own_key, extent, cuts, -0.22, 0.18)
    return jnp.clip(result, -bound, bound).astype(held_as)


def setup_inputs(seed: int = 0) -> dict:
    streams_of = jax.random.split(jax.random.key(seed), 11)
    return {
        "hidden": draw_hidden(jax.random.fold_in(streams_of[10], 71), 0),
        "norm_gain": jnp.clip(1.0 + 0.18 * jax.random.normal(streams_of[1], (MODEL_WIDTH,), jnp.float32), 0.1, 1.9),
        "w_query": bell_draw(streams_of[2], (MODEL_WIDTH, QUERY_HEADS * HEAD_WIDTH), MODEL_WIDTH ** -0.5, 0.0625, ((0, 4), (1, 8))),
        "key_weight_matrix": bell_draw(streams_of[3], (MODEL_WIDTH, KEY_VALUE_HEADS * HEAD_WIDTH), MODEL_WIDTH ** -0.5, 0.0625, ((0, 4),)),
        "value_weight_matrix": bell_draw(streams_of[4], (MODEL_WIDTH, KEY_VALUE_HEADS * HEAD_WIDTH), MODEL_WIDTH ** -0.5, 0.0625, ((0, 4),)),
        "cache_key": draw_cache_key(jax.random.fold_in(streams_of[10], 71), 0),
        "prefix_value_cache": bell_draw(streams_of[6], (PREFIX_TOKENS, KEY_VALUE_HEADS * HEAD_WIDTH), 1.0, 5.0, ((0, 4),)),
        "start": jax.random.randint(streams_of[7], (1,), PREFIX_TOKENS, CONTEXT - WINDOW + 1).astype(jnp.int32),
        "reach": plant(jax.random.randint(streams_of[8], (NB, BT), 0, PREFIX_TOKENS + WINDOW), jax.random.fold_in(streams_of[8], 1), 0, (PREFIX_TOKENS + WINDOW) - 1).astype(jnp.int32),
        "passkey": plant(jax.random.randint(streams_of[9], (NPASS,), 0, PREFIX_TOKENS), jax.random.fold_in(streams_of[9], 1), 0, PREFIX_TOKENS - 1).astype(jnp.int32),
    }


rope_base = 500000.0
yarn_factor = 8.0
trained_context = 8192.0
fast_turns = 32.0
slow_turns = 1.0
masked_score = -1e+30

def yarn_tables(positions, head_size):
    half = head_size // 2
    log_base = math.log(rope_base)
    lowest = math.floor(head_size * math.log(trained_context / (fast_turns * 2.0 * math.pi)) / (2.0 * log_base))
    highest = math.ceil(head_size * math.log(trained_context / (slow_turns * 2.0 * math.pi)) / (2.0 * log_base))
    spread = max(highest - lowest, 1)
    counter = jnp.arange(half, dtype=jnp.float32)
    inverse = jnp.exp(-(2.0 * counter / head_size) * log_base)
    ramp = jnp.clip((counter - lowest) / spread, 0.0, 1.0)
    mixed = inverse / yarn_factor * ramp + inverse * (1.0 - ramp)
    angles = positions.astype(jnp.float32)[:, None] * mixed[None, :]
    mscale = 0.1 * math.log(yarn_factor) + 1.0
    return (jnp.cos(angles) * mscale, jnp.sin(angles) * mscale)

def apply_rotary(matrix, heads, cosine_table, sine_table):
    count = matrix.shape[0]
    shaped = matrix.reshape(count, heads, -1)
    half = shaped.shape[2] // 2
    front = shaped[:, :, :half]
    back = shaped[:, :, half:]
    cosine_table = cosine_table[:, None, :]
    sine_table = sine_table[:, None, :]
    turned = jnp.concatenate([front * cosine_table - back * sine_table, back * cosine_table + front * sine_table], axis=2)
    return turned.reshape(count, heads * 2 * half)

def reference(hidden, norm_gain, w_query, key_weight_matrix, value_weight_matrix, cache_key, prefix_value_cache, start, reach, passkey):
    tokens = hidden.reshape(WINDOW, MODEL_WIDTH).astype(jnp.float32)
    inv_rms = lax.rsqrt(lax.optimization_barrier(jnp.mean(tokens * tokens, axis=1, keepdims=True)) + 1e-05)
    normed = (tokens * inv_rms * norm_gain[None, :]).astype(jnp.bfloat16)
    query_raw = jnp.dot(normed, w_query, preferred_element_type=jnp.float32)
    unrotated_key = jnp.dot(normed, key_weight_matrix, preferred_element_type=jnp.float32)
    value_raw = jnp.dot(normed, value_weight_matrix, preferred_element_type=jnp.float32)
    positions = start[0] + jnp.arange(WINDOW, dtype=jnp.int32)
    cosine_table, sine_table = yarn_tables(positions, HEAD_WIDTH)
    query = apply_rotary(query_raw, QUERY_HEADS, cosine_table, sine_table).astype(jnp.bfloat16)
    window_key_rows = apply_rotary(unrotated_key, KEY_VALUE_HEADS, cosine_table, sine_table).astype(jnp.bfloat16)
    value_new = value_raw.astype(jnp.bfloat16)
    keys_all = jnp.concatenate([cache_key, window_key_rows], axis=0)
    values_all = jnp.concatenate([prefix_value_cache, value_new], axis=0)
    key_index = jnp.arange(PREFIX_TOKENS + WINDOW, dtype=jnp.int32)
    query_index = PREFIX_TOKENS + jnp.arange(WINDOW, dtype=jnp.int32)
    cache_index = jnp.arange(PREFIX_TOKENS, dtype=jnp.int32)
    pinned_cache = jnp.any(cache_index[:, None] == passkey[None, :], axis=1)
    pinned = jnp.concatenate([pinned_cache, jnp.zeros((WINDOW,), dtype=bool)], axis=0)
    reach_flat = reach.reshape(WINDOW)
    visible = (key_index[None, :] <= query_index[:, None]) & ((key_index[None, :] >= query_index[:, None] - reach_flat[:, None]) | pinned[None, :])
    query_group = QUERY_HEADS // KEY_VALUE_HEADS
    inv_sqrt = 1.0 / math.sqrt(HEAD_WIDTH)

    def one_head(head):
        query_head = lax.dynamic_slice_in_dim(query, head * HEAD_WIDTH, HEAD_WIDTH, 1)
        kv_index = head // query_group
        key_head = lax.dynamic_slice_in_dim(keys_all, kv_index * HEAD_WIDTH, HEAD_WIDTH, 1)
        head_of_value = lax.dynamic_slice_in_dim(values_all, kv_index * HEAD_WIDTH, HEAD_WIDTH, 1)
        scores = lax.dot_general(query_head, key_head, (((1,), (1,)), ((), ())), preferred_element_type=jnp.float32) * inv_sqrt
        scores = jnp.where(visible, scores, masked_score)
        largest = lax.optimization_barrier(jnp.max(scores, axis=1, keepdims=True))
        weights = jnp.where(visible, jnp.exp(scores - largest), 0.0)
        total = lax.optimization_barrier(jnp.sum(weights, axis=1, keepdims=True))
        mixed = jnp.dot(weights.astype(jnp.bfloat16), head_of_value, preferred_element_type=jnp.float32)
        return (mixed / total).astype(jnp.bfloat16)
    heads_out = lax.map(one_head, jnp.arange(QUERY_HEADS, dtype=jnp.int32))
    return heads_out.transpose(1, 0, 2).reshape(NB, BT, QUERY_HEADS * HEAD_WIDTH)
```

```python
import functools
import math

import jax
import jax.numpy as jnp
from jax import lax
from jax.experimental import pallas as pl
from jax.experimental.pallas import tpu as pltpu
from jax.sharding import PartitionSpec as P

QUERY_HEADS = 64
KEY_VALUE_HEADS = 8
HEAD_WIDTH = 128
MEBI = 1024 * 1024
CHUNKS = 2

rope_base = 500000.0
yarn_factor = 8.0
trained_context = 8192.0
fast_turns = 32.0
slow_turns = 1.0
masked_score = -1e30
lowest_max = -1e29
F32 = jnp.float32
BF16 = jnp.bfloat16


def yarn_tables(positions, head_size):
    half = head_size // 2
    log_base = math.log(rope_base)
    lowest = math.floor(
        head_size * math.log(trained_context / (fast_turns * 2.0 * math.pi)) / (2.0 * log_base)
    )
    highest = math.ceil(
        head_size * math.log(trained_context / (slow_turns * 2.0 * math.pi)) / (2.0 * log_base)
    )
    spread = max(highest - lowest, 1)
    counter = jnp.arange(half, dtype=jnp.float32)
    inverse = jnp.exp(-(2.0 * counter / head_size) * log_base)
    ramp = jnp.clip((counter - lowest) / spread, 0.0, 1.0)
    mixed = inverse / yarn_factor * ramp + inverse * (1.0 - ramp)
    angles = positions.astype(jnp.float32)[:, None] * mixed[None, :]
    mscale = 0.1 * math.log(yarn_factor) + 1.0
    return (jnp.cos(angles) * mscale, jnp.sin(angles) * mscale)


def swapped(block, axis, mask):
    return lax.ppermute(block, axis, [(i, i ^ mask) for i in range(lax.axis_size(axis))])


def params(*arrays):
    held = sum(math.prod(a.shape) * jnp.dtype(a.dtype).itemsize for a in arrays)
    return pltpu.CompilerParams(vmem_limit_bytes=min(56 * MEBI, 4 * MEBI + held))


def vmem(count=1):
    return [pl.BlockSpec(memory_space=pltpu.VMEM)] * count


def smem():
    return pl.BlockSpec(memory_space=pltpu.SMEM)


def norm_kernel(ids, hidden, gain, reach, *rest):
    outs, scratch = rest[:-1], rest[-1]
    rows, width = outs[0].shape
    x = hidden[0].astype(F32)
    inv_rms = lax.rsqrt(jnp.mean(x * x, axis=1, keepdims=True) + 1e-05)
    scratch[...] = x * inv_rms * gain[...]
    digits = jnp.concatenate([reach[...] >> 7, reach[...] & 127], axis=1).astype(F32)
    digits = jnp.broadcast_to(digits, (rows, digits.shape[1])).astype(BF16)
    for d, out in enumerate(outs):
        at = pl.multiple_of((ids[0] ^ d) * width, width)
        out[:, :width] = scratch[:, pl.ds(at, width)].astype(BF16)
        if out.shape[1] > width:
            out[:, width:] = digits


def norm(ids, hidden, gain, reach, blocks):
    _, rows, features = hidden.shape
    width = features // blocks
    longer = width + 2 * reach.shape[1]
    widths = [longer if d and d % 2 == 0 else width for d in range(blocks)]
    return pl.pallas_call(
        norm_kernel,
        out_shape=[jax.ShapeDtypeStruct((rows, size), BF16) for size in widths],
        in_specs=[smem()] + vmem(3),
        out_specs=vmem(blocks),
        scratch_shapes=[pltpu.VMEM((rows, features), F32)],
        compiler_params=params(hidden, gain),
        name="norm",
    )(ids, hidden, gain, reach)


def prepare_kernel(keys, values, out):
    out[0] = keys[...]
    for at in range(0, values.shape[0], HEAD_WIDTH):
        part = values[at : at + HEAD_WIDTH].astype(F32)
        out[1, at : at + HEAD_WIDTH] = part.T.astype(BF16)


def prepare(keys, values):
    return pl.pallas_call(
        prepare_kernel,
        in_specs=vmem(2),
        out_specs=vmem()[0],
        out_shape=jax.ShapeDtypeStruct((2, *keys.shape), BF16),
        compiler_params=pltpu.CompilerParams(vmem_limit_bytes=6 * MEBI),
        name="prepare",
    )(keys, values)


def mask_kernel(cached, groups, ids, passkey, low, bias):
    half, count = low.shape
    rows = count // groups
    total = 2 * cached
    lows = jnp.concatenate([low[j : j + 1] for j in range(half)], axis=1)
    lanes = half * count

    def index_of(slot, block):
        token = ((slot // rows) ^ ids[1]) * rows + slot % rows
        return ids[3] + block * count + token

    step = min(256, cached)
    ramp = lax.broadcasted_iota(jnp.int32, (step, lanes), 0)
    for side in range(2):
        first = (ids[0] ^ side) * cached
        for at in range(0, cached, step):
            here = side * cached + at
            bias[here : here + step] = jnp.where(ramp >= lows - (first + at), 0.0, masked_score)
        for n in range(passkey.shape[0]):
            row = passkey[n] - first

            @pl.when((row >= 0) & (row < cached))
            def _():
                bias[pl.ds(side * cached + row, 1), :] = jnp.zeros((1, lanes), F32)

    slots = lax.broadcasted_iota(jnp.int32, (1, count), 1)
    queries = jnp.concatenate([index_of(slots, ids[0] ^ (2 * j)) for j in range(half)], axis=1)
    slots = lax.broadcasted_iota(jnp.int32, (count, 1), 0)
    for d in range(2):
        index = index_of(slots, ids[0] ^ d)
        bias[total + d * count : total + (d + 1) * count] = jnp.where(
            (index <= queries) & (index >= lows), 0.0, masked_score
        )


def mask(ids, passkey, low, cached, groups):
    half, count = low.shape
    shape = jax.ShapeDtypeStruct((2 * cached + 2 * count, half * count), F32)
    return pl.pallas_call(
        functools.partial(mask_kernel, cached, groups),
        out_shape=shape,
        in_specs=[smem(), smem()] + vmem(),
        out_specs=vmem()[0],
        compiler_params=params(shape),
        name="mask",
    )(ids, passkey, low)


def gather_kernel(groups, part, *refs):
    pieces = refs[:groups]
    weights, tokens, keep, send = refs[groups:]
    blocks, rows, width = pieces[0].shape
    count = groups * rows
    pair = 2 * HEAD_WIDTH
    for d in range(blocks):
        block = jnp.concatenate([piece[d].astype(F32) for piece in pieces], axis=0)
        tokens[d * count : (d + 1) * count] = block.astype(BF16)
    raw = jnp.dot(tokens[...], weights[:, part:], preferred_element_type=F32)
    for d in range(blocks):
        block = raw[d * count : (d + 1) * count]
        first, other = (send, keep) if d % 2 else (keep, send)
        first[d // 2, :, part : part + pair] = block
        other[d // 2, :, part + pair :] = block
    tile = min(256, part)
    for at in range(0, part, tile):
        raw = jnp.dot(tokens[...], weights[:, at : at + tile], preferred_element_type=F32)
        for d in range(blocks):
            out = send if d % 2 else keep
            out[d // 2, :, at : at + tile] = raw[d * count : (d + 1) * count]


def gather(pieces, weights, part):
    groups = len(pieces)
    blocks, rows, width = pieces[0].shape
    count = groups * rows
    columns = part + 4 * HEAD_WIDTH
    tokens = jax.ShapeDtypeStruct((blocks * count, width), BF16)
    out = jax.ShapeDtypeStruct((blocks // 2, count, columns), F32)
    return pl.pallas_call(
        functools.partial(gather_kernel, groups, part),
        out_shape=[tokens, out, out],
        in_specs=vmem(groups + 1),
        out_specs=vmem(3),
        compiler_params=params(tokens, tokens, weights, out, out),
        cost_estimate=pl.CostEstimate(
            flops=2 * blocks * count * width * columns,
            bytes_accessed=4 * blocks * count * width,
            transcendentals=0,
        ),
        name="gather",
    )(*pieces, weights)


def project_kernel(tokens, weights, keep, send):
    half, count, _ = keep.shape
    raw = jnp.dot(tokens[...], weights[...], preferred_element_type=F32)
    for j in range(half):
        keep[j] = raw[2 * j * count : (2 * j + 1) * count]
        send[j] = raw[(2 * j + 1) * count : (2 * j + 2) * count]


def project(tokens, weights, blocks, at, columns):
    rows, width = tokens.shape
    tile = min(256, columns)
    half, count = blocks // 2, rows // blocks
    out = jax.ShapeDtypeStruct((half, count, columns), F32)
    out_spec = pl.BlockSpec((half, count, tile), lambda n: (0, 0, n))
    return pl.pallas_call(
        project_kernel,
        grid=(columns // tile,),
        in_specs=[
            pl.BlockSpec((rows, width), lambda n: (0, 0)),
            pl.BlockSpec((width, tile), lambda n: (0, n + at // tile)),
        ],
        out_specs=[out_spec, out_spec],
        out_shape=[out, out],
        compiler_params=params(tokens, tokens, out, out, out, out),
        cost_estimate=pl.CostEstimate(
            flops=2 * rows * width * columns,
            bytes_accessed=2 * width * columns,
            transcendentals=0,
        ),
        name="project",
    )(tokens, weights)


def turned(x, cosine, sine):
    return x * cosine + pltpu.roll(x, HEAD_WIDTH // 2, 1) * sine


def attend_kernel(together, q, kv, cosine, sine, bias, own, far, _, o_keep,
                   o_send, stats_keep, scores, k_new, v_new, pair, arrived):
    fetch = pltpu.make_async_copy(far, pair, arrived)
    fetch.start()
    half, count, columns = q.shape
    rows = half * count
    cached = own.shape[1]
    window = 2 * count
    heads = columns // HEAD_WIDTH
    for d in range(2):
        raw = kv[d]
        k_new[d * count : (d + 1) * count] = turned(
            raw[:, :HEAD_WIDTH], cosine[d], sine[d]
        ).astype(BF16)
    values = jnp.concatenate([kv[d, :, HEAD_WIDTH:] for d in range(2)], axis=0)
    for at in range(0, window, HEAD_WIDTH):
        v_new[at : at + HEAD_WIDTH] = values[at : at + HEAD_WIDTH].T.astype(BF16)
    scale = math.log2(math.e) / math.sqrt(HEAD_WIDTH)
    chunk = min(256, cached)
    spans = [
        (base + at, chunk, held.at[0], held.at[1], at)
        for held, base in ((own, 0), (pair, cached))
        for at in range(0, cached, chunk)
    ]
    spans += [
        (2 * cached + at, HEAD_WIDTH, k_new, v_new, at) for at in range(0, window, HEAD_WIDTH)
    ]
    width = together * rows
    tops, sums = [], []
    for first in range(0, heads, together):
        queries = []
        for h in range(first, first + together):
            lanes = slice(h * HEAD_WIDTH, (h + 1) * HEAD_WIDTH)
            for j in range(half):
                queries.append(turned(q[j, :, lanes], cosine[2 * j], sine[2 * j]).astype(BF16))
        queries = jnp.concatenate(queries, axis=0)
        top = jnp.full((8, width), lowest_max, F32)
        for at, size, keys, _, start in spans:
            if first == 0 and at == cached:
                fetch.wait()
            product = lax.dot_general(
                keys[start : start + size],
                queries,
                (((1,), (1,)), ((), ())),
                preferred_element_type=F32,
            )
            hidden_part = bias[at : at + size]
            product = product * scale + jnp.concatenate([hidden_part] * together, axis=1)
            scores[at : at + size] = product
            top = jnp.maximum(top, jnp.max(product.reshape(size // 8, 8, width), axis=0))
        top = jnp.max(top, axis=0, keepdims=True)
        total = jnp.zeros((8, width), F32)
        mixed = jnp.zeros((HEAD_WIDTH, width), F32)
        for at, size, _, held, start in spans:
            weights = jnp.exp2(scores[at : at + size] - top)
            total = total + jnp.sum(weights.reshape(size // 8, 8, width), axis=0)
            turned_values = jnp.concatenate(
                [held[start + c : start + c + HEAD_WIDTH] for c in range(0, size, HEAD_WIDTH)],
                axis=1,
            )
            mixed = mixed + jnp.dot(
                turned_values, weights.astype(BF16), preferred_element_type=F32
            )
        total = jnp.sum(total, axis=0, keepdims=True)
        mixed = mixed * (1.0 / jnp.maximum(total, 1e-30))
        for n in range(together):
            lanes = slice((first + n) * HEAD_WIDTH, (first + n + 1) * HEAD_WIDTH)
            tops.append(top[:, n * rows : (n + 1) * rows])
            sums.append(total[:, n * rows : (n + 1) * rows])
            upright = mixed[:, n * rows : (n + 1) * rows].T
            for j in range(half):
                part = upright[j * count : (j + 1) * count]
                if j < half // 2:
                    o_keep[j, :, lanes] = part
                else:
                    o_send[j - half // 2, :, lanes] = part.astype(BF16)
    stats = jnp.concatenate(tops + sums, axis=0)
    number = stats.shape[0]
    high = stats.astype(BF16).astype(F32)
    middle = (stats - high).astype(BF16).astype(F32)
    last = stats - high - middle
    stats = jnp.concatenate(
        [high, middle, last, jnp.zeros((HEAD_WIDTH - 3 * number, rows), F32)], axis=0
    ).T
    for j in range(half):
        part = stats[j * count : (j + 1) * count]
        if j < half // 2:
            stats_keep[j] = part
        else:
            o_send[j - half // 2, :, columns:] = part.astype(BF16)


def attend(q, kv, cosine, sine, bias, own, pair, before):
    half, count, columns = q.shape
    rows = half * count
    total = bias.shape[0]
    heads = columns // HEAD_WIDTH
    together = max(1, min(512 // rows, heads))
    out_half = half // 2
    outs = [
        jax.ShapeDtypeStruct((out_half, count, columns), F32),
        jax.ShapeDtypeStruct((out_half, count, columns + HEAD_WIDTH), BF16),
        jax.ShapeDtypeStruct((out_half, count, HEAD_WIDTH), F32),
    ]
    ins = (q, kv, cosine, sine, bias, own, pair, before)
    scores = jax.ShapeDtypeStruct((total, together * rows), F32)
    return pl.pallas_call(
        functools.partial(attend_kernel, together),
        out_shape=outs,
        in_specs=vmem(len(ins) - 2) + [pl.BlockSpec(memory_space=pl.ANY)] * 2,
        out_specs=vmem(3),
        scratch_shapes=[
            pltpu.VMEM(scores.shape, F32),
            pltpu.VMEM((2 * count, HEAD_WIDTH), BF16),
            pltpu.VMEM((2 * count, HEAD_WIDTH), BF16),
            pltpu.VMEM(pair.shape, BF16),
            pltpu.SemaphoreType.DMA(()),
        ],
        compiler_params=params(*ins, *outs, scores),
        cost_estimate=pl.CostEstimate(
            flops=16 * rows * columns * total,
            bytes_accessed=4 * rows * columns * 4,
            transcendentals=rows * heads * total,
        ),
        name="attend",
    )(*ins)


def merged(mine, other, mine_stats):
    columns = mine.shape[1]
    heads = columns // HEAD_WIDTH

    def read(stats):
        number = 2 * heads
        stats = (
            stats[:, :number] + stats[:, number : 2 * number] + stats[:, 2 * number : 3 * number]
        )
        return stats[:, :heads], stats[:, heads:]

    top_a, sum_a = read(mine_stats)
    top_b, sum_b = read(other[:, columns:].astype(F32))
    top = jnp.maximum(top_a, top_b)
    share_a = sum_a * jnp.exp2(top_a - top)
    share_b = sum_b * jnp.exp2(top_b - top)
    total = share_a + share_b
    scale = 1.0 / jnp.maximum(total, 1e-30)
    share_a = share_a * scale
    share_b = share_b * scale
    joined = [
        mine[:, h * HEAD_WIDTH : (h + 1) * HEAD_WIDTH] * share_a[:, h : h + 1]
        + other[:, h * HEAD_WIDTH : (h + 1) * HEAD_WIDTH].astype(F32) * share_b[:, h : h + 1]
        for h in range(heads)
    ]
    return joined, top, total


def merge_kernel(mine, other, mine_stats, keep, send, stats_keep):
    blocks, count, columns = mine.shape
    half = blocks // 2
    for n in range(blocks):
        joined, top, total = merged(mine[n], other[n], mine_stats[n])
        stats = jnp.concatenate([top, total], axis=1)
        high = stats.astype(BF16).astype(F32)
        middle = (stats - high).astype(BF16).astype(F32)
        number = stats.shape[1]
        stats = jnp.concatenate(
            [
                high,
                middle,
                stats - high - middle,
                jnp.zeros((count, HEAD_WIDTH - 3 * number), F32),
            ],
            axis=1,
        )
        for h, part in enumerate(joined):
            lanes = slice(h * HEAD_WIDTH, (h + 1) * HEAD_WIDTH)
            if n < half:
                keep[n, :, lanes] = part
            else:
                send[n - half, :, lanes] = part.astype(BF16)
        if n < half:
            stats_keep[n] = stats
        else:
            send[n - half, :, columns:] = stats.astype(BF16)


def merge(mine, other, mine_stats):
    blocks, count, columns = mine.shape
    half = blocks // 2
    return pl.pallas_call(
        merge_kernel,
        out_shape=[
            jax.ShapeDtypeStruct((half, count, columns), F32),
            jax.ShapeDtypeStruct((half, count, columns + HEAD_WIDTH), BF16),
            jax.ShapeDtypeStruct((half, count, HEAD_WIDTH), F32),
        ],
        in_specs=vmem(3),
        out_specs=vmem(3),
        compiler_params=params(mine, mine, other, mine_stats),
        name="merge",
    )(mine, other, mine_stats)


def finish_kernel(chunks, ids, *refs):
    out = refs[-1]
    groups, rows, _ = out.shape
    at = 0
    for c in range(chunks):
        mine, other, stats = refs[3 * c : 3 * c + 3]
        joined, _, _ = merged(mine[0], other[0], stats[0])
        for part in joined:
            for m in range(groups):
                out[ids[1] ^ m, :, at : at + HEAD_WIDTH] = part[m * rows : (m + 1) * rows].astype(
                    BF16
                )
            at += HEAD_WIDTH


def finish(ids, parts, groups):
    count = parts[0][0].shape[1]
    columns = sum(part[0].shape[2] for part in parts)
    flat = [array for part in parts for array in part]
    return pl.pallas_call(
        functools.partial(finish_kernel, len(parts)),
        out_shape=jax.ShapeDtypeStruct((groups, count // groups, columns), BF16),
        in_specs=[smem()] + vmem(len(flat)),
        out_specs=vmem()[0],
        compiler_params=params(*flat),
        name="finish",
    )(ids, *flat)


def reordered(array, flip):
    if not flip:
        return array
    return jnp.stack([array[j ^ flip] for j in range(array.shape[0])])


def local(
    hidden,
    norm_gain,
    w_query,
    key_weight_matrix,
    value_weight_matrix,
    cache_key,
    prefix_value_cache,
    start,
    reach,
    passkey,
):
    blocks = lax.axis_size("blk")
    groups = lax.axis_size("wide")
    b = lax.axis_index("blk").astype(jnp.int32)
    w = lax.axis_index("wide").astype(jnp.int32)
    rows, features = hidden.shape[1:]
    count = groups * rows
    half = blocks // 2
    heads = QUERY_HEADS // groups
    columns = w_query.shape[1]
    chunks = min(CHUNKS, heads)
    kv_head = w * heads // (QUERY_HEADS // KEY_VALUE_HEADS)
    cached = cache_key.shape[0]
    cache_total = cached * blocks
    ids = jnp.stack([b, w, kv_head, jnp.int32(cache_total)])
    largest = 1.9 * 0.0625 * features * 1.01
    fit = 2.0 ** math.floor(math.log2(65504.0 / largest))

    def narrow(array):
        return (array * fit).astype(jnp.float16)

    def widen(array):
        return array.astype(F32) * (1.0 / fit)

    slices = norm(ids, hidden, norm_gain[None, :], reach, blocks)
    sent = [swapped(slices[d], "blk", d) for d in range(1, blocks)]
    slices, cache_key, prefix_value_cache = lax.optimization_barrier(
        (slices, cache_key, prefix_value_cache)
    )
    base = kv_head * HEAD_WIDTH
    cache = prepare(
        lax.dynamic_slice_in_dim(cache_key, base, HEAD_WIDTH, 1),
        lax.dynamic_slice_in_dim(prefix_value_cache, base, HEAD_WIDTH, 1),
    )
    cache_pair = swapped(cache, "blk", 1)
    width = features // blocks
    own = jnp.stack([slices[0]] + [array[:, :width] for array in sent])
    own, first_weights, key_weight_matrix, value_weight_matrix = lax.optimization_barrier(
        (own, w_query, key_weight_matrix, value_weight_matrix)
    )

    pieces = [None] * groups
    for m in range(0, groups, 2):
        pieces[m] = swapped(own, "wide", m) if m else own
    for m in range(0, groups, 2):
        pieces[m + 1] = swapped(pieces[m], "wide", 1)

    weights = jnp.concatenate(
        [
            first_weights[:, : columns // chunks],
            lax.dynamic_slice_in_dim(key_weight_matrix, base, HEAD_WIDTH, 1),
            lax.dynamic_slice_in_dim(value_weight_matrix, base, HEAD_WIDTH, 1),
        ],
        axis=1,
    )

    token = (w ^ jnp.arange(groups, dtype=jnp.int32))[:, None] * rows + jnp.arange(
        rows, dtype=jnp.int32
    )
    token = token.reshape(count)
    block_of = b ^ jnp.arange(blocks, dtype=jnp.int32)
    place = block_of[:, None] * count + token[None, :]
    cosine, sine = yarn_tables(start[0] + place.reshape(-1), HEAD_WIDTH)
    cosine = jnp.concatenate([cosine, cosine], axis=1).reshape(blocks, count, HEAD_WIDTH)
    sine = jnp.concatenate([-sine, sine], axis=1).reshape(blocks, count, HEAD_WIDTH)
    digits = [array[0, width:].astype(jnp.int32) for array in sent[1::2]]
    reaches = jnp.stack(
        [reach[0]] + [array[:count] * 128 + array[count:] for array in digits]
    )
    natural = jnp.arange(count, dtype=jnp.int32)
    reaches = jnp.sum(
        jnp.where(token[None, :, None] == natural[None, None, :], reaches[:, None, :], 0), axis=2
    )
    bias = mask(ids, passkey, cache_total + place[::2] - reaches, cached, groups)

    part = columns // chunks
    tokens, *first = gather(pieces, weights, part)
    projected = [first] + [
        project(tokens, w_query, blocks, c * part, part) for c in range(1, chunks)
    ]
    pair = 2 * HEAD_WIDTH
    parts = []
    got = [swapped(narrow(send), "blk", 1) for _, send in projected]
    after = cosine
    for c, (keep, _) in enumerate(projected):
        keep = keep + widen(got[c])
        if c == 0:
            even = keep[:, :, part : part + pair]
            odd = keep[:, :, part + pair :]
            keep = keep[:, :, :part]
        bit = half // 2
        while bit >= 1:
            out = narrow(keep)
            if c == 0:
                extra = narrow(jnp.concatenate([even[bit:], odd[bit:]], axis=0))
                even, odd = even[:bit], odd[:bit]
                if 2 * bit == half:
                    out = jnp.concatenate([out, extra], axis=2)
                    other = swapped(out, "blk", 2 * bit)
                    other, extra = other[:, :, :part], other[:, :, part:]
                else:
                    other = swapped(out, "blk", 2 * bit)
                    extra = swapped(extra, "blk", 2 * bit)
                even = even + widen(extra[:bit])
                odd = odd + widen(extra[bit:])
            else:
                other = swapped(out, "blk", 2 * bit)
            keep = keep + reordered(widen(other), bit)
            bit //= 2
        if c == 0:
            kv = jnp.concatenate([even, odd], axis=0)
        keep, send, stats = attend(keep, kv, cosine, sine, bias, cache, cache_pair, after)
        after = stats
        bit = half // 2
        while bit > 1:
            keep, send, stats = merge(keep, swapped(send, "blk", 2 * bit), stats)
            bit //= 2
        parts.append((keep, swapped(send, "blk", 2), stats))
    ready = finish(ids, parts, groups)
    ready = lax.all_to_all(ready, "wide", split_axis=0, concat_axis=0, tiled=True)
    return ready.transpose(1, 0, 2).reshape(1, rows, groups * columns)


def solution(mesh):
    return jax.shard_map(
        local,
        mesh=mesh,
        in_specs=(
            P("blk", "wide", None),
            P(),
            P("blk", "wide"),
            P("blk", None),
            P("blk", None),
            P("blk", None),
            P("blk", None),
            P(),
            P("blk", None),
            P(),
        ),
        out_specs=P("blk", "wide", None),
        check_vma=False,
    )
```

```python
import functools
import math

import jax
import jax.numpy as jnp
from jax import lax
from jax.experimental import pallas as pl
from jax.experimental.pallas import tpu as pltpu
from jax.sharding import PartitionSpec as P

QUERY_HEADS = 64
KEY_VALUE_HEADS = 8
HEAD_WIDTH = 128
MEBI = 1024 * 1024
CHUNKS = 2

rope_base = 500000.0
yarn_factor = 8.0
trained_context = 8192.0
fast_turns = 32.0
slow_turns = 1.0
masked_score = -1e30
lowest_max = -1e29
F32 = jnp.float32
BF16 = jnp.bfloat16


def yarn_tables(positions, head_size):
    half = head_size // 2
    log_base = math.log(rope_base)
    lowest = math.floor(
        head_size * math.log(trained_context / (fast_turns * 2.0 * math.pi)) / (2.0 * log_base)
    )
    highest = math.ceil(
        head_size * math.log(trained_context / (slow_turns * 2.0 * math.pi)) / (2.0 * log_base)
    )
    spread = max(highest - lowest, 1)
    lane = jnp.arange(head_size, dtype=jnp.int32)
    counter = (lane % half).astype(jnp.float32)
    inverse = jnp.exp(-(2.0 * counter / head_size) * log_base)
    ramp = jnp.clip((counter - lowest) / spread, 0.0, 1.0)
    mixed = inverse / yarn_factor * ramp + inverse * (1.0 - ramp)
    angles = positions.astype(jnp.float32) * mixed
    mscale = 0.1 * math.log(yarn_factor) + 1.0
    signed = jnp.where(lane < half, -mscale, mscale)
    return (jnp.cos(angles) * mscale, jnp.sin(angles) * signed)


def swapped(block, axis, mask):
    return lax.ppermute(block, axis, [(i, i ^ mask) for i in range(lax.axis_size(axis))])


def params(*arrays):
    held = sum(math.prod(a.shape) * jnp.dtype(a.dtype).itemsize for a in arrays)
    return pltpu.CompilerParams(vmem_limit_bytes=min(56 * MEBI, 4 * MEBI + held))


def vmem(count=1):
    return [pl.BlockSpec(memory_space=pltpu.VMEM)] * count


def smem():
    return pl.BlockSpec(memory_space=pltpu.SMEM)


def norm_kernel(hidden, gain, reach, *rest):
    outs, scratch = rest[:-1], rest[-1]
    rows, width = outs[0].shape
    me = lax.axis_index("blk")
    x = hidden[0].astype(F32)
    inv_rms = lax.rsqrt(jnp.mean(x * x, axis=1, keepdims=True) + 1e-05)
    scratch[...] = x * inv_rms * gain[...]
    digits = jnp.concatenate([reach[...] >> 7, reach[...] & 127], axis=1).astype(F32)
    digits = jnp.broadcast_to(digits, (rows, digits.shape[1])).astype(BF16)
    for d, out in enumerate(outs):
        at = pl.multiple_of((me ^ d) * width, width)
        out[:, :width] = scratch[:, pl.ds(at, width)].astype(BF16)
        if out.shape[1] > width:
            out[:, width:] = digits


def norm(hidden, gain, reach, blocks):
    _, rows, features = hidden.shape
    width = features // blocks
    longer = width + 2 * reach.shape[1]
    widths = [longer if d and d % 2 == 0 else width for d in range(blocks)]
    return pl.pallas_call(
        norm_kernel,
        out_shape=[jax.ShapeDtypeStruct((rows, size), BF16) for size in widths],
        in_specs=vmem(3),
        out_specs=vmem(blocks),
        scratch_shapes=[pltpu.VMEM((rows, features), F32)],
        compiler_params=pltpu.CompilerParams(vmem_limit_bytes=56 * MEBI),
        name="norm",
    )(hidden, gain, reach)


def prepare_kernel(keys, values, out):
    out[0] = keys[...]
    for at in range(0, values.shape[0], HEAD_WIDTH):
        part = values[at : at + HEAD_WIDTH].astype(F32)
        out[1, at : at + HEAD_WIDTH] = part.T.astype(BF16)


def prepare(keys, values):
    return pl.pallas_call(
        prepare_kernel,
        in_specs=vmem(2),
        out_specs=vmem()[0],
        out_shape=jax.ShapeDtypeStruct((2, *keys.shape), BF16),
        compiler_params=pltpu.CompilerParams(vmem_limit_bytes=6 * MEBI),
        name="prepare",
    )(keys, values)


def mask_kernel(cached, groups, ids, passkey, reach, *refs):
    digits, bias = refs[:-1], refs[-1]
    half = len(digits) + 1
    count = reach.shape[1]
    rows = count // groups
    total = 2 * cached
    lanes = half * count

    def token_of(slot):
        return ((slot // rows) ^ ids[1]) * rows + slot % rows

    slots = lax.broadcasted_iota(jnp.int32, (1, count), 1)
    tokens = token_of(slots)
    down = lax.broadcasted_iota(jnp.int32, (count, count), 0)
    across = lax.broadcasted_iota(jnp.int32, (count, count), 1)
    reaches = [reach[...].astype(F32)]
    for array in digits:
        pair = array[:1].astype(F32)
        reaches.append(pair[:, :count] * 128.0 + pair[:, count:])
    lows, queries = [], []
    for j, natural in enumerate(reaches):
        column = jnp.sum(jnp.where(down == across, natural, 0.0), axis=1, keepdims=True)
        slotted = jnp.sum(jnp.where(down == tokens, column, 0.0), axis=0, keepdims=True)
        index = ids[3] + (ids[0] ^ (2 * j)) * count + tokens
        queries.append(index)
        lows.append(index - slotted.astype(jnp.int32))
    lows = jnp.concatenate(lows, axis=1)
    queries = jnp.concatenate(queries, axis=1)

    step = min(256, cached)
    ramp = lax.broadcasted_iota(jnp.int32, (step, lanes), 0)
    for side in range(2):
        first = (ids[0] ^ side) * cached
        for at in range(0, cached, step):
            here = side * cached + at
            bias[here : here + step] = jnp.where(ramp >= lows - (first + at), 0.0, masked_score)
        for n in range(passkey.shape[0]):
            row = passkey[n] - first

            @pl.when((row >= 0) & (row < cached))
            def _():
                bias[pl.ds(side * cached + row, 1), :] = jnp.zeros((1, lanes), F32)

    slots = lax.broadcasted_iota(jnp.int32, (count, 1), 0)
    for d in range(2):
        index = ids[3] + (ids[0] ^ d) * count + token_of(slots)
        bias[total + d * count : total + (d + 1) * count] = jnp.where(
            (index <= queries) & (index >= lows), 0.0, masked_score
        )


def mask(ids, passkey, reach, digits, cached, groups):
    count = reach.shape[1]
    half = len(digits) + 1
    shape = jax.ShapeDtypeStruct((2 * cached + 2 * count, half * count), F32)
    return pl.pallas_call(
        functools.partial(mask_kernel, cached, groups),
        out_shape=shape,
        in_specs=[smem(), smem()] + vmem(half),
        out_specs=vmem()[0],
        compiler_params=params(shape),
        name="mask",
    )(ids, passkey, reach, *digits)


def gather_kernel(groups, part, *refs):
    pieces = refs[:groups]
    weights, tokens, keep, send = refs[groups:]
    blocks, rows, width = pieces[0].shape
    count = groups * rows
    pair = 2 * HEAD_WIDTH
    for d in range(blocks):
        block = jnp.concatenate([piece[d].astype(F32) for piece in pieces], axis=0)
        tokens[d * count : (d + 1) * count] = block.astype(BF16)
    raw = jnp.dot(tokens[...], weights[:, part:], preferred_element_type=F32)
    for d in range(blocks):
        block = raw[d * count : (d + 1) * count]
        first, other = (send, keep) if d % 2 else (keep, send)
        first[d // 2, :, part : part + pair] = block
        other[d // 2, :, part + pair :] = block
    tile = min(256, part)
    for at in range(0, part, tile):
        raw = jnp.dot(tokens[...], weights[:, at : at + tile], preferred_element_type=F32)
        for d in range(blocks):
            out = send if d % 2 else keep
            out[d // 2, :, at : at + tile] = raw[d * count : (d + 1) * count]


def gather(pieces, weights, part):
    groups = len(pieces)
    blocks, rows, width = pieces[0].shape
    count = groups * rows
    columns = part + 4 * HEAD_WIDTH
    tokens = jax.ShapeDtypeStruct((blocks * count, width), BF16)
    out = jax.ShapeDtypeStruct((blocks // 2, count, columns), F32)
    return pl.pallas_call(
        functools.partial(gather_kernel, groups, part),
        out_shape=[tokens, out, out],
        in_specs=vmem(groups + 1),
        out_specs=vmem(3),
        compiler_params=params(tokens, tokens, weights, out, out),
        cost_estimate=pl.CostEstimate(
            flops=2 * blocks * count * width * columns,
            bytes_accessed=4 * blocks * count * width,
            transcendentals=0,
        ),
        name="gather",
    )(*pieces, weights)


def project_kernel(tokens, weights, keep, send):
    half, count, _ = keep.shape
    raw = jnp.dot(tokens[...], weights[...], preferred_element_type=F32)
    for j in range(half):
        keep[j] = raw[2 * j * count : (2 * j + 1) * count]
        send[j] = raw[(2 * j + 1) * count : (2 * j + 2) * count]


def project(tokens, weights, blocks, at, columns):
    rows, width = tokens.shape
    tile = min(256, columns)
    half, count = blocks // 2, rows // blocks
    out = jax.ShapeDtypeStruct((half, count, columns), F32)
    out_spec = pl.BlockSpec((half, count, tile), lambda n: (0, 0, n))
    return pl.pallas_call(
        project_kernel,
        grid=(columns // tile,),
        in_specs=[
            pl.BlockSpec((rows, width), lambda n: (0, 0)),
            pl.BlockSpec((width, tile), lambda n: (0, n + at // tile)),
        ],
        out_specs=[out_spec, out_spec],
        out_shape=[out, out],
        compiler_params=params(tokens, tokens, out, out, out, out),
        cost_estimate=pl.CostEstimate(
            flops=2 * rows * width * columns,
            bytes_accessed=2 * width * columns,
            transcendentals=0,
        ),
        name="project",
    )(tokens, weights)


def turned(x, cosine, sine):
    return x * cosine + pltpu.roll(x, HEAD_WIDTH // 2, 1) * sine


def attend_kernel(together, q, kv, cosine, sine, bias, own, far, o_keep,
                   o_send, stats_keep, scores, k_new, v_new, pair, arrived):
    fetch = pltpu.make_async_copy(far, pair, arrived)
    fetch.start()
    half, count, columns = q.shape
    rows = half * count
    cached = own.shape[1]
    window = 2 * count
    heads = columns // HEAD_WIDTH
    for d in range(2):
        raw = kv[d]
        k_new[d * count : (d + 1) * count] = turned(
            raw[:, :HEAD_WIDTH], cosine[d], sine[d]
        ).astype(BF16)
    values = jnp.concatenate([kv[d, :, HEAD_WIDTH:] for d in range(2)], axis=0)
    for at in range(0, window, HEAD_WIDTH):
        v_new[at : at + HEAD_WIDTH] = values[at : at + HEAD_WIDTH].T.astype(BF16)
    scale = math.log2(math.e) / math.sqrt(HEAD_WIDTH)
    chunk = min(256, cached)
    spans = [
        (base + at, chunk, held.at[0], held.at[1], at)
        for held, base in ((own, 0), (pair, cached))
        for at in range(0, cached, chunk)
    ]
    spans += [
        (2 * cached + at, HEAD_WIDTH, k_new, v_new, at) for at in range(0, window, HEAD_WIDTH)
    ]
    width = together * rows
    tops, sums = [], []
    for first in range(0, heads, together):
        queries = []
        for h in range(first, first + together):
            lanes = slice(h * HEAD_WIDTH, (h + 1) * HEAD_WIDTH)
            for j in range(half):
                queries.append(turned(q[j, :, lanes], cosine[2 * j], sine[2 * j]).astype(BF16))
        queries = jnp.concatenate(queries, axis=0)
        top = jnp.full((8, width), lowest_max, F32)
        for at, size, keys, _, start in spans:
            if first == 0 and at == cached:
                fetch.wait()
            product = lax.dot_general(
                keys[start : start + size],
                queries,
                (((1,), (1,)), ((), ())),
                preferred_element_type=F32,
            )
            hidden_part = bias[at : at + size]
            product = product * scale + jnp.concatenate([hidden_part] * together, axis=1)
            scores[at : at + size] = product
            top = jnp.maximum(top, jnp.max(product.reshape(size // 8, 8, width), axis=0))
        top = jnp.max(top, axis=0, keepdims=True)
        total = jnp.zeros((8, width), F32)
        mixed = jnp.zeros((HEAD_WIDTH, width), F32)
        for at, size, _, held, start in spans:
            weights = jnp.exp2(scores[at : at + size] - top)
            total = total + jnp.sum(weights.reshape(size // 8, 8, width), axis=0)
            turned_values = jnp.concatenate(
                [held[start + c : start + c + HEAD_WIDTH] for c in range(0, size, HEAD_WIDTH)],
                axis=1,
            )
            mixed = mixed + jnp.dot(
                turned_values, weights.astype(BF16), preferred_element_type=F32
            )
        total = jnp.sum(total, axis=0, keepdims=True)
        mixed = mixed * (1.0 / jnp.maximum(total, 1e-30))
        for n in range(together):
            lanes = slice((first + n) * HEAD_WIDTH, (first + n + 1) * HEAD_WIDTH)
            tops.append(top[:, n * rows : (n + 1) * rows])
            sums.append(total[:, n * rows : (n + 1) * rows])
            upright = mixed[:, n * rows : (n + 1) * rows].T
            for j in range(half):
                part = upright[j * count : (j + 1) * count]
                if j < half // 2:
                    o_keep[j, :, lanes] = part
                else:
                    o_send[j - half // 2, :, lanes] = part.astype(BF16)
    stats = jnp.concatenate(tops + sums, axis=0)
    number = stats.shape[0]
    high = stats.astype(BF16).astype(F32)
    middle = (stats - high).astype(BF16).astype(F32)
    last = stats - high - middle
    stats = jnp.concatenate(
        [high, middle, last, jnp.zeros((HEAD_WIDTH - 3 * number, rows), F32)], axis=0
    ).T
    for j in range(half):
        part = stats[j * count : (j + 1) * count]
        if j < half // 2:
            stats_keep[j] = part
        else:
            o_send[j - half // 2, :, columns:] = part.astype(BF16)


def attend(q, kv, cosine, sine, bias, own, pair):
    half, count, columns = q.shape
    rows = half * count
    total = bias.shape[0]
    heads = columns // HEAD_WIDTH
    together = max(1, min(512 // rows, heads))
    out_half = half // 2
    outs = [
        jax.ShapeDtypeStruct((out_half, count, columns), F32),
        jax.ShapeDtypeStruct((out_half, count, columns + HEAD_WIDTH), BF16),
        jax.ShapeDtypeStruct((out_half, count, HEAD_WIDTH), F32),
    ]
    ins = (q, kv, cosine, sine, bias, own, pair)
    scores = jax.ShapeDtypeStruct((total, together * rows), F32)
    return pl.pallas_call(
        functools.partial(attend_kernel, together),
        out_shape=outs,
        in_specs=vmem(len(ins) - 1) + [pl.BlockSpec(memory_space=pl.ANY)],
        out_specs=vmem(3),
        scratch_shapes=[
            pltpu.VMEM(scores.shape, F32),
            pltpu.VMEM((2 * count, HEAD_WIDTH), BF16),
            pltpu.VMEM((2 * count, HEAD_WIDTH), BF16),
            pltpu.VMEM(pair.shape, BF16),
            pltpu.SemaphoreType.DMA(()),
        ],
        compiler_params=params(*ins, *outs, scores),
        cost_estimate=pl.CostEstimate(
            flops=16 * rows * columns * total,
            bytes_accessed=4 * rows * columns * 4,
            transcendentals=rows * heads * total,
        ),
        name="attend",
    )(*ins)


def merged(mine, other, mine_stats):
    columns = mine.shape[1]
    heads = columns // HEAD_WIDTH

    def read(stats):
        number = 2 * heads
        stats = (
            stats[:, :number] + stats[:, number : 2 * number] + stats[:, 2 * number : 3 * number]
        )
        return stats[:, :heads], stats[:, heads:]

    top_a, sum_a = read(mine_stats)
    top_b, sum_b = read(other[:, columns:].astype(F32))
    top = jnp.maximum(top_a, top_b)
    share_a = sum_a * jnp.exp2(top_a - top)
    share_b = sum_b * jnp.exp2(top_b - top)
    total = share_a + share_b
    scale = 1.0 / jnp.maximum(total, 1e-30)
    share_a = share_a * scale
    share_b = share_b * scale
    joined = [
        mine[:, h * HEAD_WIDTH : (h + 1) * HEAD_WIDTH] * share_a[:, h : h + 1]
        + other[:, h * HEAD_WIDTH : (h + 1) * HEAD_WIDTH].astype(F32) * share_b[:, h : h + 1]
        for h in range(heads)
    ]
    return joined, top, total


def merge_kernel(mine, other, mine_stats, keep, send, stats_keep):
    blocks, count, columns = mine.shape
    half = blocks // 2
    for n in range(blocks):
        joined, top, total = merged(mine[n], other[n], mine_stats[n])
        stats = jnp.concatenate([top, total], axis=1)
        high = stats.astype(BF16).astype(F32)
        middle = (stats - high).astype(BF16).astype(F32)
        number = stats.shape[1]
        stats = jnp.concatenate(
            [
                high,
                middle,
                stats - high - middle,
                jnp.zeros((count, HEAD_WIDTH - 3 * number), F32),
            ],
            axis=1,
        )
        for h, part in enumerate(joined):
            lanes = slice(h * HEAD_WIDTH, (h + 1) * HEAD_WIDTH)
            if n < half:
                keep[n, :, lanes] = part
            else:
                send[n - half, :, lanes] = part.astype(BF16)
        if n < half:
            stats_keep[n] = stats
        else:
            send[n - half, :, columns:] = stats.astype(BF16)


def merge(mine, other, mine_stats):
    blocks, count, columns = mine.shape
    half = blocks // 2
    return pl.pallas_call(
        merge_kernel,
        out_shape=[
            jax.ShapeDtypeStruct((half, count, columns), F32),
            jax.ShapeDtypeStruct((half, count, columns + HEAD_WIDTH), BF16),
            jax.ShapeDtypeStruct((half, count, HEAD_WIDTH), F32),
        ],
        in_specs=vmem(3),
        out_specs=vmem(3),
        compiler_params=params(mine, mine, other, mine_stats),
        name="merge",
    )(mine, other, mine_stats)


def finish_kernel(chunks, ids, *refs):
    out = refs[-1]
    groups, rows, _ = out.shape
    at = 0
    for c in range(chunks):
        mine, other, stats = refs[3 * c : 3 * c + 3]
        joined, _, _ = merged(mine[0], other[0], stats[0])
        for part in joined:
            for m in range(groups):
                out[ids[1] ^ m, :, at : at + HEAD_WIDTH] = part[m * rows : (m + 1) * rows].astype(
                    BF16
                )
            at += HEAD_WIDTH


def finish(ids, parts, groups):
    count = parts[0][0].shape[1]
    columns = sum(part[0].shape[2] for part in parts)
    flat = [array for part in parts for array in part]
    return pl.pallas_call(
        functools.partial(finish_kernel, len(parts)),
        out_shape=jax.ShapeDtypeStruct((groups, count // groups, columns), BF16),
        in_specs=[smem()] + vmem(len(flat)),
        out_specs=vmem()[0],
        compiler_params=params(*flat),
        name="finish",
    )(ids, *flat)


def reordered(array, flip):
    if not flip:
        return array
    return jnp.stack([array[j ^ flip] for j in range(array.shape[0])])


def local(
    hidden,
    norm_gain,
    w_query,
    key_weight_matrix,
    value_weight_matrix,
    cache_key,
    prefix_value_cache,
    start,
    reach,
    passkey,
):
    blocks = lax.axis_size("blk")
    groups = lax.axis_size("wide")
    b = lax.axis_index("blk").astype(jnp.int32)
    w = lax.axis_index("wide").astype(jnp.int32)
    rows, features = hidden.shape[1:]
    count = groups * rows
    half = blocks // 2
    heads = QUERY_HEADS // groups
    columns = w_query.shape[1]
    chunks = min(CHUNKS, heads)
    kv_head = w * heads // (QUERY_HEADS // KEY_VALUE_HEADS)
    cached = cache_key.shape[0]
    cache_total = cached * blocks
    ids = jnp.stack([b, w, kv_head, jnp.int32(cache_total)])
    largest = 1.9 * 0.0625 * features * 1.01
    fit = 2.0 ** math.floor(math.log2(65504.0 / largest))

    def narrow(array):
        return (array * fit).astype(jnp.float16)

    def widen(array):
        return array.astype(F32) * (1.0 / fit)

    slices = norm(hidden, norm_gain[None, :], reach, blocks)
    sent = [swapped(slices[d], "blk", d) for d in range(1, blocks)]
    slices, cache_key, prefix_value_cache = lax.optimization_barrier(
        (slices, cache_key, prefix_value_cache)
    )
    base = kv_head * HEAD_WIDTH
    cache = prepare(
        lax.dynamic_slice_in_dim(cache_key, base, HEAD_WIDTH, 1),
        lax.dynamic_slice_in_dim(prefix_value_cache, base, HEAD_WIDTH, 1),
    )
    cache_pair = swapped(cache, "blk", 1)
    width = features // blocks
    own = jnp.stack([slices[0]] + [array[:, :width] for array in sent])
    own, first_weights, key_weight_matrix, value_weight_matrix = lax.optimization_barrier(
        (own, w_query, key_weight_matrix, value_weight_matrix)
    )

    pieces = [None] * groups
    for m in range(0, groups, 2):
        pieces[m] = swapped(own, "wide", m) if m else own
    for m in range(0, groups, 2):
        pieces[m + 1] = swapped(pieces[m], "wide", 1)

    weights = jnp.concatenate(
        [
            first_weights[:, : columns // chunks],
            lax.dynamic_slice_in_dim(key_weight_matrix, base, HEAD_WIDTH, 1),
            lax.dynamic_slice_in_dim(value_weight_matrix, base, HEAD_WIDTH, 1),
        ],
        axis=1,
    )

    shape = (blocks, count, HEAD_WIDTH)
    slot = lax.broadcasted_iota(jnp.int32, shape, 1)
    block = b ^ lax.broadcasted_iota(jnp.int32, shape, 0)
    token = ((slot // rows) ^ w) * rows + slot % rows
    cosine, sine = yarn_tables(start[0] + block * count + token, HEAD_WIDTH)
    digits = [array[:, width:] for array in sent[1::2]]
    bias = mask(ids, passkey, reach, digits, cached, groups)

    part = columns // chunks
    tokens, *first = gather(pieces, weights, part)
    projected = [first] + [
        project(tokens, w_query, blocks, c * part, part) for c in range(1, chunks)
    ]
    pair = 2 * HEAD_WIDTH
    order = list(range(chunks))
    got = {c: swapped(narrow(projected[c][1]), "blk", 1) for c in order}
    queries = {}
    for c in order:
        keep = projected[c][0] + widen(got[c])
        if c == 0:
            even = keep[:, :, part : part + pair]
            odd = keep[:, :, part + pair :]
            keep = keep[:, :, :part]
        bit = half // 2
        while bit >= 1:
            out = narrow(keep)
            if c == 0:
                extra = narrow(jnp.concatenate([even[bit:], odd[bit:]], axis=0))
                even, odd = even[:bit], odd[:bit]
                if 2 * bit == half:
                    out = jnp.concatenate([out, extra], axis=2)
                    other = swapped(out, "blk", 2 * bit)
                    other, extra = other[:, :, :part], other[:, :, part:]
                else:
                    other = swapped(out, "blk", 2 * bit)
                    extra = swapped(extra, "blk", 2 * bit)
                even = even + widen(extra[:bit])
                odd = odd + widen(extra[bit:])
            else:
                other = swapped(out, "blk", 2 * bit)
            keep = keep + reordered(widen(other), bit)
            bit //= 2
        if c == 0:
            kv = jnp.concatenate([even, odd], axis=0)
        queries[c] = keep
    parts = {}
    for c in range(chunks):
        keep, send, stats = attend(queries[c], kv, cosine, sine, bias, cache, cache_pair)
        bit = half // 2
        while bit > 1:
            keep, send, stats = merge(keep, swapped(send, "blk", 2 * bit), stats)
            bit //= 2
        parts[c] = (keep, swapped(send, "blk", 2), stats)
    parts = [parts[c] for c in range(chunks)]
    ready = finish(ids, parts, groups)
    ready = lax.all_to_all(ready, "wide", split_axis=0, concat_axis=0, tiled=True)
    return ready.transpose(1, 0, 2).reshape(1, rows, groups * columns)


def solution(mesh):
    return jax.shard_map(
        local,
        mesh=mesh,
        in_specs=(
            P("blk", "wide", None),
            P(),
            P("blk", "wide"),
            P("blk", None),
            P("blk", None),
            P("blk", None),
            P("blk", None),
            P(),
            P("blk", None),
            P(),
        ),
        out_specs=P("blk", "wide", None),
        check_vma=False,
    )
```

```python
import functools
import math

import jax
import jax.numpy as jnp
from jax import lax
from jax.experimental import pallas as pl
from jax.experimental.pallas import tpu as pltpu
from jax.sharding import PartitionSpec as P

QUERY_HEADS = 64
KEY_VALUE_HEADS = 8
HEAD_WIDTH = 128
MEBI = 1024 * 1024
CHUNKS = 2

rope_base = 500000.0
yarn_factor = 8.0
trained_context = 8192.0
fast_turns = 32.0
slow_turns = 1.0
masked_score = -1e30
lowest_max = -1e29
F32 = jnp.float32
BF16 = jnp.bfloat16


def yarn_tables(positions, head_size):
    half = head_size // 2
    log_base = math.log(rope_base)
    lowest = math.floor(
        head_size * math.log(trained_context / (fast_turns * 2.0 * math.pi)) / (2.0 * log_base)
    )
    highest = math.ceil(
        head_size * math.log(trained_context / (slow_turns * 2.0 * math.pi)) / (2.0 * log_base)
    )
    spread = max(highest - lowest, 1)
    lane = jnp.arange(head_size, dtype=jnp.int32)
    counter = (lane % half).astype(jnp.float32)
    inverse = jnp.exp(-(2.0 * counter / head_size) * log_base)
    ramp = jnp.clip((counter - lowest) / spread, 0.0, 1.0)
    mixed = inverse / yarn_factor * ramp + inverse * (1.0 - ramp)
    angles = positions.astype(jnp.float32) * mixed
    mscale = 0.1 * math.log(yarn_factor) + 1.0
    signed = jnp.where(lane < half, -mscale, mscale)
    return (jnp.cos(angles) * mscale, jnp.sin(angles) * signed)


def swapped(block, axis, mask):
    return lax.ppermute(block, axis, [(i, i ^ mask) for i in range(lax.axis_size(axis))])


def params(*arrays):
    held = sum(math.prod(a.shape) * jnp.dtype(a.dtype).itemsize for a in arrays)
    return pltpu.CompilerParams(vmem_limit_bytes=min(56 * MEBI, 4 * MEBI + held))


def vmem(count=1):
    return [pl.BlockSpec(memory_space=pltpu.VMEM)] * count


def smem():
    return pl.BlockSpec(memory_space=pltpu.SMEM)


def norm_kernel(hidden, gain, reach, *rest):
    outs, scratch = rest[:-1], rest[-1]
    rows, width = outs[0].shape
    me = lax.axis_index("blk")
    x = hidden[0].astype(F32)
    inv_rms = lax.rsqrt(jnp.mean(x * x, axis=1, keepdims=True) + 1e-05)
    scratch[...] = x * inv_rms * gain[...]
    digits = jnp.concatenate([reach[...] >> 7, reach[...] & 127], axis=1).astype(F32)
    digits = jnp.broadcast_to(digits, (rows, digits.shape[1])).astype(BF16)
    for d, out in enumerate(outs):
        at = pl.multiple_of((me ^ d) * width, width)
        out[:, :width] = scratch[:, pl.ds(at, width)].astype(BF16)
        if out.shape[1] > width:
            out[:, width:] = digits


def norm(hidden, gain, reach, blocks):
    _, rows, features = hidden.shape
    width = features // blocks
    longer = width + 2 * reach.shape[1]
    widths = [longer if d and d % 2 == 0 else width for d in range(blocks)]
    return pl.pallas_call(
        norm_kernel,
        out_shape=[jax.ShapeDtypeStruct((rows, size), BF16) for size in widths],
        in_specs=vmem(3),
        out_specs=vmem(blocks),
        scratch_shapes=[pltpu.VMEM((rows, features), F32)],
        compiler_params=pltpu.CompilerParams(vmem_limit_bytes=56 * MEBI),
        name="norm",
    )(hidden, gain, reach)


def prepare_kernel(keys, values, out, first):
    size = first.shape[1]
    out[0] = keys[...]
    first[0] = keys[:size]
    for at in range(0, values.shape[0], HEAD_WIDTH):
        part = values[at : at + HEAD_WIDTH].astype(F32).T.astype(BF16)
        out[1, at : at + HEAD_WIDTH] = part
        if at < size:
            first[1, at : at + HEAD_WIDTH] = part


def prepare(keys, values, size):
    return pl.pallas_call(
        prepare_kernel,
        in_specs=vmem(2),
        out_specs=vmem(2),
        out_shape=[
            jax.ShapeDtypeStruct((2, *keys.shape), BF16),
            jax.ShapeDtypeStruct((2, size, keys.shape[1]), BF16),
        ],
        compiler_params=pltpu.CompilerParams(vmem_limit_bytes=6 * MEBI),
        name="prepare",
    )(keys, values)


def rest_kernel(held, *refs):
    out = refs[-1]
    size = out.shape[1]
    out[...] = held[:, held.shape[1] - size :]


def rest(held, size, earlier):
    return pl.pallas_call(
        rest_kernel,
        in_specs=vmem(1) + [pl.BlockSpec(memory_space=pl.ANY)] * len(earlier),
        out_specs=vmem()[0],
        out_shape=jax.ShapeDtypeStruct((2, size, held.shape[2]), BF16),
        compiler_params=pltpu.CompilerParams(vmem_limit_bytes=6 * MEBI),
        name="rest",
    )(held, *earlier)


def mask_kernel(cached, groups, ids, passkey, reach, *refs):
    digits, bias = refs[:-1], refs[-1]
    half = len(digits) + 1
    count = reach.shape[1]
    rows = count // groups
    total = 2 * cached
    lanes = half * count

    def token_of(slot):
        return ((slot // rows) ^ ids[1]) * rows + slot % rows

    slots = lax.broadcasted_iota(jnp.int32, (1, count), 1)
    tokens = token_of(slots)
    down = lax.broadcasted_iota(jnp.int32, (count, count), 0)
    across = lax.broadcasted_iota(jnp.int32, (count, count), 1)
    reaches = [reach[...].astype(F32)]
    for array in digits:
        pair = array[:1].astype(F32)
        reaches.append(pair[:, :count] * 128.0 + pair[:, count:])
    lows, queries = [], []
    for j, natural in enumerate(reaches):
        column = jnp.sum(jnp.where(down == across, natural, 0.0), axis=1, keepdims=True)
        slotted = jnp.sum(jnp.where(down == tokens, column, 0.0), axis=0, keepdims=True)
        index = ids[3] + (ids[0] ^ (2 * j)) * count + tokens
        queries.append(index)
        lows.append(index - slotted.astype(jnp.int32))
    lows = jnp.concatenate(lows, axis=1)
    queries = jnp.concatenate(queries, axis=1)

    step = min(256, cached)
    ramp = lax.broadcasted_iota(jnp.int32, (step, lanes), 0)
    for side in range(2):
        first = (ids[0] ^ side) * cached
        for at in range(0, cached, step):
            here = side * cached + at
            bias[here : here + step] = jnp.where(ramp >= lows - (first + at), 0.0, masked_score)
        for n in range(passkey.shape[0]):
            row = passkey[n] - first

            @pl.when((row >= 0) & (row < cached))
            def _():
                bias[pl.ds(side * cached + row, 1), :] = jnp.zeros((1, lanes), F32)

    slots = lax.broadcasted_iota(jnp.int32, (count, 1), 0)
    for d in range(2):
        index = ids[3] + (ids[0] ^ d) * count + token_of(slots)
        bias[total + d * count : total + (d + 1) * count] = jnp.where(
            (index <= queries) & (index >= lows), 0.0, masked_score
        )


def mask(ids, passkey, reach, digits, cached, groups):
    count = reach.shape[1]
    half = len(digits) + 1
    shape = jax.ShapeDtypeStruct((2 * cached + 2 * count, half * count), F32)
    return pl.pallas_call(
        functools.partial(mask_kernel, cached, groups),
        out_shape=shape,
        in_specs=[smem(), smem()] + vmem(half),
        out_specs=vmem()[0],
        compiler_params=params(shape),
        name="mask",
    )(ids, passkey, reach, *digits)


def gather_kernel(groups, part, *refs):
    pieces = refs[:groups]
    weights, tokens, keep, send = refs[groups:]
    blocks, rows, width = pieces[0].shape
    count = groups * rows
    pair = 2 * HEAD_WIDTH
    for d in range(blocks):
        block = jnp.concatenate([piece[d].astype(F32) for piece in pieces], axis=0)
        tokens[d * count : (d + 1) * count] = block.astype(BF16)
    raw = jnp.dot(tokens[...], weights[:, part:], preferred_element_type=F32)
    for d in range(blocks):
        block = raw[d * count : (d + 1) * count]
        first, other = (send, keep) if d % 2 else (keep, send)
        first[d // 2, :, part : part + pair] = block
        other[d // 2, :, part + pair :] = block
    tile = min(256, part)
    for at in range(0, part, tile):
        raw = jnp.dot(tokens[...], weights[:, at : at + tile], preferred_element_type=F32)
        for d in range(blocks):
            out = send if d % 2 else keep
            out[d // 2, :, at : at + tile] = raw[d * count : (d + 1) * count]


def gather(pieces, weights, part):
    groups = len(pieces)
    blocks, rows, width = pieces[0].shape
    count = groups * rows
    columns = part + 4 * HEAD_WIDTH
    tokens = jax.ShapeDtypeStruct((blocks * count, width), BF16)
    out = jax.ShapeDtypeStruct((blocks // 2, count, columns), F32)
    return pl.pallas_call(
        functools.partial(gather_kernel, groups, part),
        out_shape=[tokens, out, out],
        in_specs=vmem(groups + 1),
        out_specs=vmem(3),
        compiler_params=params(tokens, tokens, weights, out, out),
        cost_estimate=pl.CostEstimate(
            flops=2 * blocks * count * width * columns,
            bytes_accessed=4 * blocks * count * width,
            transcendentals=0,
        ),
        name="gather",
    )(*pieces, weights)


def project_kernel(tokens, weights, keep, send):
    half, count, _ = keep.shape
    raw = jnp.dot(tokens[...], weights[...], preferred_element_type=F32)
    for j in range(half):
        keep[j] = raw[2 * j * count : (2 * j + 1) * count]
        send[j] = raw[(2 * j + 1) * count : (2 * j + 2) * count]


def project(tokens, weights, blocks, at, columns):
    rows, width = tokens.shape
    tile = min(256, columns)
    half, count = blocks // 2, rows // blocks
    out = jax.ShapeDtypeStruct((half, count, columns), F32)
    out_spec = pl.BlockSpec((half, count, tile), lambda n: (0, 0, n))
    return pl.pallas_call(
        project_kernel,
        grid=(columns // tile,),
        in_specs=[
            pl.BlockSpec((rows, width), lambda n: (0, 0)),
            pl.BlockSpec((width, tile), lambda n: (0, n + at // tile)),
        ],
        out_specs=[out_spec, out_spec],
        out_shape=[out, out],
        compiler_params=params(tokens, tokens, out, out, out, out),
        cost_estimate=pl.CostEstimate(
            flops=2 * rows * width * columns,
            bytes_accessed=2 * width * columns,
            transcendentals=0,
        ),
        name="project",
    )(tokens, weights)


def turned(x, cosine, sine):
    return x * cosine + pltpu.roll(x, HEAD_WIDTH // 2, 1) * sine


def attend_kernel(together, q, kv, cosine, sine, bias, own, far_first, far_last, o_keep,
                   o_send, stats_keep, scores, k_new, v_new, pair, arrived):
    early = far_first.shape[1]
    fetches = {}
    for n, (far, at) in enumerate(((far_first, 0), (far_last, early))):
        for side in range(2):
            fetch = pltpu.make_async_copy(
                far.at[side], pair.at[side, pl.ds(at, far.shape[1])], arrived.at[2 * n + side]
            )
            fetch.start()
            fetches.setdefault(own.shape[1] + at, []).append(fetch)
    half, count, columns = q.shape
    rows = half * count
    cached = own.shape[1]
    window = 2 * count
    heads = columns // HEAD_WIDTH
    for d in range(2):
        raw = kv[d]
        k_new[d * count : (d + 1) * count] = turned(
            raw[:, :HEAD_WIDTH], cosine[d], sine[d]
        ).astype(BF16)
    values = jnp.concatenate([kv[d, :, HEAD_WIDTH:] for d in range(2)], axis=0)
    for at in range(0, window, HEAD_WIDTH):
        v_new[at : at + HEAD_WIDTH] = values[at : at + HEAD_WIDTH].T.astype(BF16)
    scale = math.log2(math.e) / math.sqrt(HEAD_WIDTH)
    chunk = min(256, cached // 2)
    spans = [
        (base + at, chunk, held.at[0], held.at[1], at)
        for held, base in ((own, 0), (pair, cached))
        for at in range(0, cached, chunk)
    ]
    spans += [
        (2 * cached + at, HEAD_WIDTH, k_new, v_new, at) for at in range(0, window, HEAD_WIDTH)
    ]
    width = together * rows
    tops, sums = [], []
    for first in range(0, heads, together):
        queries = []
        for h in range(first, first + together):
            lanes = slice(h * HEAD_WIDTH, (h + 1) * HEAD_WIDTH)
            for j in range(half):
                queries.append(turned(q[j, :, lanes], cosine[2 * j], sine[2 * j]).astype(BF16))
        queries = jnp.concatenate(queries, axis=0)
        top = jnp.full((8, width), lowest_max, F32)
        for at, size, keys, _, start in spans:
            if first == 0:
                for fetch in fetches.get(at, ()):
                    fetch.wait()
            product = lax.dot_general(
                keys[start : start + size],
                queries,
                (((1,), (1,)), ((), ())),
                preferred_element_type=F32,
            )
            hidden_part = bias[at : at + size]
            product = product * scale + jnp.concatenate([hidden_part] * together, axis=1)
            scores[at : at + size] = product
            top = jnp.maximum(top, jnp.max(product.reshape(size // 8, 8, width), axis=0))
        top = jnp.max(top, axis=0, keepdims=True)
        total = jnp.zeros((8, width), F32)
        mixed = jnp.zeros((HEAD_WIDTH, width), F32)
        for at, size, _, held, start in spans:
            weights = jnp.exp2(scores[at : at + size] - top)
            total = total + jnp.sum(weights.reshape(size // 8, 8, width), axis=0)
            turned_values = jnp.concatenate(
                [held[start + c : start + c + HEAD_WIDTH] for c in range(0, size, HEAD_WIDTH)],
                axis=1,
            )
            mixed = mixed + jnp.dot(
                turned_values, weights.astype(BF16), preferred_element_type=F32
            )
        total = jnp.sum(total, axis=0, keepdims=True)
        mixed = mixed * (1.0 / jnp.maximum(total, 1e-30))
        for n in range(together):
            lanes = slice((first + n) * HEAD_WIDTH, (first + n + 1) * HEAD_WIDTH)
            tops.append(top[:, n * rows : (n + 1) * rows])
            sums.append(total[:, n * rows : (n + 1) * rows])
            upright = mixed[:, n * rows : (n + 1) * rows].T
            for j in range(half):
                part = upright[j * count : (j + 1) * count]
                if j < half // 2:
                    o_keep[j, :, lanes] = part
                else:
                    o_send[j - half // 2, :, lanes] = part.astype(BF16)
    stats = jnp.concatenate(tops + sums, axis=0)
    number = stats.shape[0]
    high = stats.astype(BF16).astype(F32)
    middle = (stats - high).astype(BF16).astype(F32)
    last = stats - high - middle
    stats = jnp.concatenate(
        [high, middle, last, jnp.zeros((HEAD_WIDTH - 3 * number, rows), F32)], axis=0
    ).T
    for j in range(half):
        part = stats[j * count : (j + 1) * count]
        if j < half // 2:
            stats_keep[j] = part
        else:
            o_send[j - half // 2, :, columns:] = part.astype(BF16)


def attend(q, kv, cosine, sine, bias, own, first, last):
    half, count, columns = q.shape
    rows = half * count
    total = bias.shape[0]
    heads = columns // HEAD_WIDTH
    together = max(1, min(512 // rows, heads))
    out_half = half // 2
    outs = [
        jax.ShapeDtypeStruct((out_half, count, columns), F32),
        jax.ShapeDtypeStruct((out_half, count, columns + HEAD_WIDTH), BF16),
        jax.ShapeDtypeStruct((out_half, count, HEAD_WIDTH), F32),
    ]
    ins = (q, kv, cosine, sine, bias, own, first, last)
    scores = jax.ShapeDtypeStruct((total, together * rows), F32)
    return pl.pallas_call(
        functools.partial(attend_kernel, together),
        out_shape=outs,
        in_specs=vmem(len(ins) - 2) + [pl.BlockSpec(memory_space=pl.ANY)] * 2,
        out_specs=vmem(3),
        scratch_shapes=[
            pltpu.VMEM(scores.shape, F32),
            pltpu.VMEM((2 * count, HEAD_WIDTH), BF16),
            pltpu.VMEM((2 * count, HEAD_WIDTH), BF16),
            pltpu.VMEM(own.shape, BF16),
            pltpu.SemaphoreType.DMA((4,)),
        ],
        compiler_params=params(*ins, *outs, scores),
        cost_estimate=pl.CostEstimate(
            flops=16 * rows * columns * total,
            bytes_accessed=4 * rows * columns * 4,
            transcendentals=rows * heads * total,
        ),
        name="attend",
    )(*ins)


def merged(mine, other, mine_stats):
    columns = mine.shape[1]
    heads = columns // HEAD_WIDTH

    def read(stats):
        number = 2 * heads
        stats = (
            stats[:, :number] + stats[:, number : 2 * number] + stats[:, 2 * number : 3 * number]
        )
        return stats[:, :heads], stats[:, heads:]

    top_a, sum_a = read(mine_stats)
    top_b, sum_b = read(other[:, columns:].astype(F32))
    top = jnp.maximum(top_a, top_b)
    share_a = sum_a * jnp.exp2(top_a - top)
    share_b = sum_b * jnp.exp2(top_b - top)
    total = share_a + share_b
    scale = 1.0 / jnp.maximum(total, 1e-30)
    share_a = share_a * scale
    share_b = share_b * scale
    joined = [
        mine[:, h * HEAD_WIDTH : (h + 1) * HEAD_WIDTH] * share_a[:, h : h + 1]
        + other[:, h * HEAD_WIDTH : (h + 1) * HEAD_WIDTH].astype(F32) * share_b[:, h : h + 1]
        for h in range(heads)
    ]
    return joined, top, total


def merge_kernel(mine, other, mine_stats, keep, send, stats_keep):
    blocks, count, columns = mine.shape
    half = blocks // 2
    for n in range(blocks):
        joined, top, total = merged(mine[n], other[n], mine_stats[n])
        stats = jnp.concatenate([top, total], axis=1)
        high = stats.astype(BF16).astype(F32)
        middle = (stats - high).astype(BF16).astype(F32)
        number = stats.shape[1]
        stats = jnp.concatenate(
            [
                high,
                middle,
                stats - high - middle,
                jnp.zeros((count, HEAD_WIDTH - 3 * number), F32),
            ],
            axis=1,
        )
        for h, part in enumerate(joined):
            lanes = slice(h * HEAD_WIDTH, (h + 1) * HEAD_WIDTH)
            if n < half:
                keep[n, :, lanes] = part
            else:
                send[n - half, :, lanes] = part.astype(BF16)
        if n < half:
            stats_keep[n] = stats
        else:
            send[n - half, :, columns:] = stats.astype(BF16)


def merge(mine, other, mine_stats):
    blocks, count, columns = mine.shape
    half = blocks // 2
    return pl.pallas_call(
        merge_kernel,
        out_shape=[
            jax.ShapeDtypeStruct((half, count, columns), F32),
            jax.ShapeDtypeStruct((half, count, columns + HEAD_WIDTH), BF16),
            jax.ShapeDtypeStruct((half, count, HEAD_WIDTH), F32),
        ],
        in_specs=vmem(3),
        out_specs=vmem(3),
        compiler_params=params(mine, mine, other, mine_stats),
        name="merge",
    )(mine, other, mine_stats)


def finish_kernel(chunks, ids, *refs):
    out = refs[-1]
    groups, rows, _ = out.shape
    at = 0
    for c in range(chunks):
        mine, other, stats = refs[3 * c : 3 * c + 3]
        joined, _, _ = merged(mine[0], other[0], stats[0])
        for part in joined:
            for m in range(groups):
                out[ids[1] ^ m, :, at : at + HEAD_WIDTH] = part[m * rows : (m + 1) * rows].astype(
                    BF16
                )
            at += HEAD_WIDTH


def finish(ids, parts, groups):
    count = parts[0][0].shape[1]
    columns = sum(part[0].shape[2] for part in parts)
    flat = [array for part in parts for array in part]
    return pl.pallas_call(
        functools.partial(finish_kernel, len(parts)),
        out_shape=jax.ShapeDtypeStruct((groups, count // groups, columns), BF16),
        in_specs=[smem()] + vmem(len(flat)),
        out_specs=vmem()[0],
        compiler_params=params(*flat),
        name="finish",
    )(ids, *flat)


def reordered(array, flip):
    if not flip:
        return array
    return jnp.stack([array[j ^ flip] for j in range(array.shape[0])])


def local(
    hidden,
    norm_gain,
    w_query,
    key_weight_matrix,
    value_weight_matrix,
    cache_key,
    prefix_value_cache,
    start,
    reach,
    passkey,
):
    blocks = lax.axis_size("blk")
    groups = lax.axis_size("wide")
    b = lax.axis_index("blk").astype(jnp.int32)
    w = lax.axis_index("wide").astype(jnp.int32)
    rows, features = hidden.shape[1:]
    count = groups * rows
    half = blocks // 2
    heads = QUERY_HEADS // groups
    columns = w_query.shape[1]
    chunks = min(CHUNKS, heads)
    kv_head = w * heads // (QUERY_HEADS // KEY_VALUE_HEADS)
    cached = cache_key.shape[0]
    cache_total = cached * blocks
    ids = jnp.stack([b, w, kv_head, jnp.int32(cache_total)])
    largest = 1.9 * 0.0625 * features * 1.01
    fit = 2.0 ** math.floor(math.log2(65504.0 / largest))

    def narrow(array):
        return (array * fit).astype(jnp.float16)

    def widen(array):
        return array.astype(F32) * (1.0 / fit)

    slices = norm(hidden, norm_gain[None, :], reach, blocks)
    sent = [swapped(slices[d], "blk", d) for d in range(1, blocks)]
    slices, cache_key, prefix_value_cache = lax.optimization_barrier(
        (slices, cache_key, prefix_value_cache)
    )
    base = kv_head * HEAD_WIDTH
    chunk = min(256, cached // 2)
    early = cached * 3 // 4 // chunk * chunk
    cache, first_rows = prepare(
        lax.dynamic_slice_in_dim(cache_key, base, HEAD_WIDTH, 1),
        lax.dynamic_slice_in_dim(prefix_value_cache, base, HEAD_WIDTH, 1),
        early,
    )
    first_rows = swapped(first_rows, "blk", 1)
    width = features // blocks
    own = jnp.stack([slices[0]] + [array[:, :width] for array in sent])
    own, first_weights, key_weight_matrix, value_weight_matrix = lax.optimization_barrier(
        (own, w_query, key_weight_matrix, value_weight_matrix)
    )

    pieces = [None] * groups
    for m in range(0, groups, 2):
        pieces[m] = swapped(own, "wide", m) if m else own
    for m in range(0, groups, 2):
        pieces[m + 1] = swapped(pieces[m], "wide", 1)

    weights = jnp.concatenate(
        [
            first_weights[:, : columns // chunks],
            lax.dynamic_slice_in_dim(key_weight_matrix, base, HEAD_WIDTH, 1),
            lax.dynamic_slice_in_dim(value_weight_matrix, base, HEAD_WIDTH, 1),
        ],
        axis=1,
    )

    shape = (blocks, count, HEAD_WIDTH)
    slot = lax.broadcasted_iota(jnp.int32, shape, 1)
    block = b ^ lax.broadcasted_iota(jnp.int32, shape, 0)
    token = ((slot // rows) ^ w) * rows + slot % rows
    cosine, sine = yarn_tables(start[0] + block * count + token, HEAD_WIDTH)
    digits = [array[:, width:] for array in sent[1::2]]
    bias = mask(ids, passkey, reach, digits, cached, groups)

    part = columns // chunks
    tokens, *first = gather(pieces, weights, part)
    projected = [first] + [
        project(tokens, w_query, blocks, c * part, part) for c in range(1, chunks)
    ]
    pair = 2 * HEAD_WIDTH
    order = list(range(chunks))
    got = {c: swapped(narrow(projected[c][1]), "blk", 1) for c in order}
    queries, sums = {}, []
    for c in order:
        keep = projected[c][0] + widen(got[c])
        sums.append(keep)
        if c == 0:
            even = keep[:, :, part : part + pair]
            odd = keep[:, :, part + pair :]
            keep = keep[:, :, :part]
        bit = half // 2
        while bit >= 1:
            out = narrow(keep)
            if c == 0:
                extra = narrow(jnp.concatenate([even[bit:], odd[bit:]], axis=0))
                even, odd = even[:bit], odd[:bit]
                if 2 * bit == half:
                    out = jnp.concatenate([out, extra], axis=2)
                    other = swapped(out, "blk", 2 * bit)
                    other, extra = other[:, :, :part], other[:, :, part:]
                else:
                    other = swapped(out, "blk", 2 * bit)
                    extra = swapped(extra, "blk", 2 * bit)
                even = even + widen(extra[:bit])
                odd = odd + widen(extra[bit:])
            else:
                other = swapped(out, "blk", 2 * bit)
            keep = keep + reordered(widen(other), bit)
            bit //= 2
        if c == 0:
            kv = jnp.concatenate([even, odd], axis=0)
        queries[c] = keep
    last_rows = swapped(rest(cache, cached - early, sums[-1:]), "blk", 1)
    parts = {}
    for c in range(chunks):
        keep, send, stats = attend(queries[c], kv, cosine, sine, bias, cache, first_rows, last_rows)
        bit = half // 2
        while bit > 1:
            keep, send, stats = merge(keep, swapped(send, "blk", 2 * bit), stats)
            bit //= 2
        parts[c] = (keep, swapped(send, "blk", 2), stats)
    parts = [parts[c] for c in range(chunks)]
    ready = finish(ids, parts, groups)
    ready = lax.all_to_all(ready, "wide", split_axis=0, concat_axis=0, tiled=True)
    return ready.transpose(1, 0, 2).reshape(1, rows, groups * columns)


def solution(mesh):
    return jax.shard_map(
        local,
        mesh=mesh,
        in_specs=(
            P("blk", "wide", None),
            P(),
            P("blk", "wide"),
            P("blk", None),
            P("blk", None),
            P("blk", None),
            P("blk", None),
            P(),
            P("blk", None),
            P(),
        ),
        out_specs=P("blk", "wide", None),
        check_vma=False,
    )
```

```python
import functools
import math

import jax
import jax.numpy as jnp
from jax import lax
from jax.experimental import pallas as pl
from jax.experimental.pallas import tpu as pltpu
from jax.sharding import PartitionSpec as P

QUERY_HEADS = 64
KEY_VALUE_HEADS = 8
HEAD_WIDTH = 128
MEBI = 1024 * 1024
CHUNKS = 2

rope_base = 500000.0
yarn_factor = 8.0
trained_context = 8192.0
fast_turns = 32.0
slow_turns = 1.0
masked_score = -1e30
lowest_max = -1e29
F32 = jnp.float32
BF16 = jnp.bfloat16


def yarn_tables(positions, head_size):
    half = head_size // 2
    log_base = math.log(rope_base)
    lowest = math.floor(
        head_size * math.log(trained_context / (fast_turns * 2.0 * math.pi)) / (2.0 * log_base)
    )
    highest = math.ceil(
        head_size * math.log(trained_context / (slow_turns * 2.0 * math.pi)) / (2.0 * log_base)
    )
    spread = max(highest - lowest, 1)
    lane = jnp.arange(head_size, dtype=jnp.int32)
    counter = (lane % half).astype(jnp.float32)
    inverse = jnp.exp(-(2.0 * counter / head_size) * log_base)
    ramp = jnp.clip((counter - lowest) / spread, 0.0, 1.0)
    mixed = inverse / yarn_factor * ramp + inverse * (1.0 - ramp)
    angles = positions.astype(jnp.float32) * mixed
    mscale = 0.1 * math.log(yarn_factor) + 1.0
    signed = jnp.where(lane < half, -mscale, mscale)
    return (jnp.cos(angles) * mscale, jnp.sin(angles) * signed)


def swapped(block, axis, mask):
    return lax.ppermute(block, axis, [(i, i ^ mask) for i in range(lax.axis_size(axis))])


def params(*arrays):
    held = sum(math.prod(a.shape) * jnp.dtype(a.dtype).itemsize for a in arrays)
    return pltpu.CompilerParams(vmem_limit_bytes=min(56 * MEBI, 4 * MEBI + held))


def vmem(count=1):
    return [pl.BlockSpec(memory_space=pltpu.VMEM)] * count


def smem():
    return pl.BlockSpec(memory_space=pltpu.SMEM)


def norm_kernel(hidden, gain, reach, *rest):
    outs, scratch = rest[:-1], rest[-1]
    rows, width = outs[0].shape
    me = lax.axis_index("blk")
    x = hidden[0].astype(F32)
    inv_rms = lax.rsqrt(jnp.mean(x * x, axis=1, keepdims=True) + 1e-05)
    scratch[...] = x * inv_rms * gain[...]
    digits = jnp.concatenate([reach[...] >> 7, reach[...] & 127], axis=1).astype(F32)
    digits = jnp.broadcast_to(digits, (rows, digits.shape[1])).astype(BF16)
    for d, out in enumerate(outs):
        at = pl.multiple_of((me ^ d) * width, width)
        out[:, :width] = scratch[:, pl.ds(at, width)].astype(BF16)
        if out.shape[1] > width:
            out[:, width:] = digits


def norm(hidden, gain, reach, blocks):
    _, rows, features = hidden.shape
    width = features // blocks
    longer = width + 2 * reach.shape[1]
    widths = [longer if d and d % 2 == 0 else width for d in range(blocks)]
    return pl.pallas_call(
        norm_kernel,
        out_shape=[jax.ShapeDtypeStruct((rows, size), BF16) for size in widths],
        in_specs=vmem(3),
        out_specs=vmem(blocks),
        scratch_shapes=[pltpu.VMEM((rows, features), F32)],
        compiler_params=pltpu.CompilerParams(vmem_limit_bytes=56 * MEBI),
        name="norm",
    )(hidden, gain, reach)


def prepare_kernel(keys, values, out, first):
    size = first.shape[1]
    out[0] = keys[...]
    first[0] = keys[:size]
    for at in range(0, values.shape[0], HEAD_WIDTH):
        part = values[at : at + HEAD_WIDTH].astype(F32).T.astype(BF16)
        out[1, at : at + HEAD_WIDTH] = part
        if at < size:
            first[1, at : at + HEAD_WIDTH] = part


def prepare(keys, values, size):
    return pl.pallas_call(
        prepare_kernel,
        in_specs=vmem(2),
        out_specs=vmem(2),
        out_shape=[
            jax.ShapeDtypeStruct((2, *keys.shape), BF16),
            jax.ShapeDtypeStruct((2, size, keys.shape[1]), BF16),
        ],
        compiler_params=pltpu.CompilerParams(vmem_limit_bytes=6 * MEBI),
        name="prepare",
    )(keys, values)


def rest_kernel(held, *refs):
    out = refs[-1]
    size = out.shape[1]
    out[...] = held[:, held.shape[1] - size :]


def rest(held, size, earlier):
    return pl.pallas_call(
        rest_kernel,
        in_specs=vmem(1) + [pl.BlockSpec(memory_space=pl.ANY)] * len(earlier),
        out_specs=vmem()[0],
        out_shape=jax.ShapeDtypeStruct((2, size, held.shape[2]), BF16),
        compiler_params=pltpu.CompilerParams(vmem_limit_bytes=6 * MEBI),
        name="rest",
    )(held, *earlier)


def mask_kernel(cached, groups, ids, passkey, reach, *refs):
    digits, bias = refs[:-1], refs[-1]
    half = len(digits) + 1
    count = reach.shape[1]
    rows = count // groups
    total = 2 * cached
    lanes = half * count

    def token_of(slot):
        return ((slot // rows) ^ ids[1]) * rows + slot % rows

    slots = lax.broadcasted_iota(jnp.int32, (1, count), 1)
    tokens = token_of(slots)
    down = lax.broadcasted_iota(jnp.int32, (count, count), 0)
    across = lax.broadcasted_iota(jnp.int32, (count, count), 1)
    reaches = [reach[...].astype(F32)]
    for array in digits:
        pair = array[:1].astype(F32)
        reaches.append(pair[:, :count] * 128.0 + pair[:, count:])
    lows, queries = [], []
    for j, natural in enumerate(reaches):
        column = jnp.sum(jnp.where(down == across, natural, 0.0), axis=1, keepdims=True)
        slotted = jnp.sum(jnp.where(down == tokens, column, 0.0), axis=0, keepdims=True)
        index = ids[3] + (ids[0] ^ (2 * j)) * count + tokens
        queries.append(index)
        lows.append(index - slotted.astype(jnp.int32))
    lows = jnp.concatenate(lows, axis=1)
    queries = jnp.concatenate(queries, axis=1)

    step = min(256, cached)
    ramp = lax.broadcasted_iota(jnp.int32, (step, lanes), 0)
    for side in range(2):
        first = (ids[0] ^ side) * cached
        for at in range(0, cached, step):
            here = side * cached + at
            bias[here : here + step] = jnp.where(ramp >= lows - (first + at), 0.0, masked_score)
        for n in range(passkey.shape[0]):
            row = passkey[n] - first

            @pl.when((row >= 0) & (row < cached))
            def _():
                bias[pl.ds(side * cached + row, 1), :] = jnp.zeros((1, lanes), F32)

    slots = lax.broadcasted_iota(jnp.int32, (count, 1), 0)
    for d in range(2):
        index = ids[3] + (ids[0] ^ d) * count + token_of(slots)
        bias[total + d * count : total + (d + 1) * count] = jnp.where(
            (index <= queries) & (index >= lows), 0.0, masked_score
        )


def mask(ids, passkey, reach, digits, cached, groups):
    count = reach.shape[1]
    half = len(digits) + 1
    shape = jax.ShapeDtypeStruct((2 * cached + 2 * count, half * count), F32)
    return pl.pallas_call(
        functools.partial(mask_kernel, cached, groups),
        out_shape=shape,
        in_specs=[smem(), smem()] + vmem(half),
        out_specs=vmem()[0],
        compiler_params=params(shape),
        name="mask",
    )(ids, passkey, reach, *digits)


def gather_kernel(groups, part, *refs):
    pieces = refs[:groups]
    weights, tokens, keep, send = refs[groups:]
    blocks, rows, width = pieces[0].shape
    count = groups * rows
    pair = 2 * HEAD_WIDTH
    for d in range(blocks):
        block = jnp.concatenate([piece[d].astype(F32) for piece in pieces], axis=0)
        tokens[d * count : (d + 1) * count] = block.astype(BF16)
    raw = jnp.dot(tokens[...], weights[:, part:], preferred_element_type=F32)
    for d in range(blocks):
        block = raw[d * count : (d + 1) * count]
        first, other = (send, keep) if d % 2 else (keep, send)
        first[d // 2, :, part : part + pair] = block
        other[d // 2, :, part + pair :] = block
    tile = min(256, part)
    for at in range(0, part, tile):
        raw = jnp.dot(tokens[...], weights[:, at : at + tile], preferred_element_type=F32)
        for d in range(blocks):
            out = send if d % 2 else keep
            out[d // 2, :, at : at + tile] = raw[d * count : (d + 1) * count]


def gather(pieces, weights, part):
    groups = len(pieces)
    blocks, rows, width = pieces[0].shape
    count = groups * rows
    columns = part + 4 * HEAD_WIDTH
    tokens = jax.ShapeDtypeStruct((blocks * count, width), BF16)
    out = jax.ShapeDtypeStruct((blocks // 2, count, columns), F32)
    return pl.pallas_call(
        functools.partial(gather_kernel, groups, part),
        out_shape=[tokens, out, out],
        in_specs=vmem(groups + 1),
        out_specs=vmem(3),
        compiler_params=params(tokens, tokens, weights, out, out),
        cost_estimate=pl.CostEstimate(
            flops=2 * blocks * count * width * columns,
            bytes_accessed=4 * blocks * count * width,
            transcendentals=0,
        ),
        name="gather",
    )(*pieces, weights)


def project_kernel(tokens, weights, keep, send):
    half, count, _ = keep.shape
    raw = jnp.dot(tokens[...], weights[...], preferred_element_type=F32)
    for j in range(half):
        keep[j] = raw[2 * j * count : (2 * j + 1) * count]
        send[j] = raw[(2 * j + 1) * count : (2 * j + 2) * count]


def project(tokens, weights, blocks, at, columns):
    rows, width = tokens.shape
    tile = min(256, columns)
    half, count = blocks // 2, rows // blocks
    out = jax.ShapeDtypeStruct((half, count, columns), F32)
    out_spec = pl.BlockSpec((half, count, tile), lambda n: (0, 0, n))
    return pl.pallas_call(
        project_kernel,
        grid=(columns // tile,),
        in_specs=[
            pl.BlockSpec((rows, width), lambda n: (0, 0)),
            pl.BlockSpec((width, tile), lambda n: (0, n + at // tile)),
        ],
        out_specs=[out_spec, out_spec],
        out_shape=[out, out],
        compiler_params=params(tokens, tokens, out, out, out, out),
        cost_estimate=pl.CostEstimate(
            flops=2 * rows * width * columns,
            bytes_accessed=2 * width * columns,
            transcendentals=0,
        ),
        name="project",
    )(tokens, weights)


def turned(x, cosine, sine):
    return x * cosine + pltpu.roll(x, HEAD_WIDTH // 2, 1) * sine


def attend_kernel(together, q, kv, cosine, sine, bias, own, far_first, far_last, o_keep,
                   o_send, stats_keep, scores, k_new, v_new, pair, arrived):
    early = far_first.shape[1]
    fetches = {}
    for n, (far, at) in enumerate(((far_first, 0), (far_last, early))):
        for side in range(2):
            fetch = pltpu.make_async_copy(
                far.at[side], pair.at[side, pl.ds(at, far.shape[1])], arrived.at[2 * n + side]
            )
            fetch.start()
            fetches.setdefault(own.shape[1] + at, []).append(fetch)
    half, count, columns = q.shape
    rows = half * count
    cached = own.shape[1]
    window = 2 * count
    heads = columns // HEAD_WIDTH
    for d in range(2):
        raw = kv[d]
        k_new[d * count : (d + 1) * count] = turned(
            raw[:, :HEAD_WIDTH], cosine[d], sine[d]
        ).astype(BF16)
    values = jnp.concatenate([kv[d, :, HEAD_WIDTH:] for d in range(2)], axis=0)
    for at in range(0, window, HEAD_WIDTH):
        v_new[at : at + HEAD_WIDTH] = values[at : at + HEAD_WIDTH].T.astype(BF16)
    scale = math.log2(math.e) / math.sqrt(HEAD_WIDTH)
    chunk = min(256, cached // 2)
    spans = [
        (base + at, chunk, held.at[0], held.at[1], at)
        for held, base in ((own, 0), (pair, cached))
        for at in range(0, cached, chunk)
    ]
    spans += [
        (2 * cached + at, HEAD_WIDTH, k_new, v_new, at) for at in range(0, window, HEAD_WIDTH)
    ]
    width = together * rows
    tops, sums = [], []
    for first in range(0, heads, together):
        queries = []
        for h in range(first, first + together):
            lanes = slice(h * HEAD_WIDTH, (h + 1) * HEAD_WIDTH)
            for j in range(half):
                queries.append(turned(q[j, :, lanes], cosine[2 * j], sine[2 * j]).astype(BF16))
        queries = jnp.concatenate(queries, axis=0)
        top = jnp.full((8, width), lowest_max, F32)
        for at, size, keys, _, start in spans:
            if first == 0:
                for fetch in fetches.get(at, ()):
                    fetch.wait()
            product = lax.dot_general(
                keys[start : start + size],
                queries,
                (((1,), (1,)), ((), ())),
                preferred_element_type=F32,
            )
            hidden_part = bias[at : at + size]
            product = product * scale + jnp.concatenate([hidden_part] * together, axis=1)
            scores[at : at + size] = product
            top = jnp.maximum(top, jnp.max(product.reshape(size // 8, 8, width), axis=0))
        top = jnp.max(top, axis=0, keepdims=True)
        total = jnp.zeros((8, width), F32)
        mixed = jnp.zeros((HEAD_WIDTH, width), F32)
        for at, size, _, held, start in spans:
            weights = jnp.exp2(scores[at : at + size] - top)
            total = total + jnp.sum(weights.reshape(size // 8, 8, width), axis=0)
            turned_values = jnp.concatenate(
                [held[start + c : start + c + HEAD_WIDTH] for c in range(0, size, HEAD_WIDTH)],
                axis=1,
            )
            mixed = mixed + jnp.dot(
                turned_values, weights.astype(BF16), preferred_element_type=F32
            )
        total = jnp.sum(total, axis=0, keepdims=True)
        mixed = mixed * (1.0 / jnp.maximum(total, 1e-30))
        for n in range(together):
            lanes = slice((first + n) * HEAD_WIDTH, (first + n + 1) * HEAD_WIDTH)
            tops.append(top[:, n * rows : (n + 1) * rows])
            sums.append(total[:, n * rows : (n + 1) * rows])
            upright = mixed[:, n * rows : (n + 1) * rows].T
            for j in range(half):
                part = upright[j * count : (j + 1) * count]
                if j < half // 2:
                    o_keep[j, :, lanes] = part
                else:
                    o_send[j - half // 2, :, lanes] = part.astype(BF16)
    stats = jnp.concatenate(tops + sums, axis=0)
    number = stats.shape[0]
    high = stats.astype(BF16).astype(F32)
    middle = (stats - high).astype(BF16).astype(F32)
    last = stats - high - middle
    stats = jnp.concatenate(
        [high, middle, last, jnp.zeros((HEAD_WIDTH - 3 * number, rows), F32)], axis=0
    ).T
    for j in range(half):
        part = stats[j * count : (j + 1) * count]
        if j < half // 2:
            stats_keep[j] = part
        else:
            o_send[j - half // 2, :, columns:] = part.astype(BF16)


def attend(q, kv, cosine, sine, bias, own, first, last):
    half, count, columns = q.shape
    rows = half * count
    total = bias.shape[0]
    heads = columns // HEAD_WIDTH
    together = max(1, min(512 // rows, heads))
    out_half = half // 2
    outs = [
        jax.ShapeDtypeStruct((out_half, count, columns), F32),
        jax.ShapeDtypeStruct((out_half, count, columns + HEAD_WIDTH), BF16),
        jax.ShapeDtypeStruct((out_half, count, HEAD_WIDTH), F32),
    ]
    ins = (q, kv, cosine, sine, bias, own, first, last)
    scores = jax.ShapeDtypeStruct((total, together * rows), F32)
    return pl.pallas_call(
        functools.partial(attend_kernel, together),
        out_shape=outs,
        in_specs=vmem(len(ins) - 2) + [pl.BlockSpec(memory_space=pl.ANY)] * 2,
        out_specs=vmem(3),
        scratch_shapes=[
            pltpu.VMEM(scores.shape, F32),
            pltpu.VMEM((2 * count, HEAD_WIDTH), BF16),
            pltpu.VMEM((2 * count, HEAD_WIDTH), BF16),
            pltpu.VMEM(own.shape, BF16),
            pltpu.SemaphoreType.DMA((4,)),
        ],
        compiler_params=params(*ins, *outs, scores),
        cost_estimate=pl.CostEstimate(
            flops=16 * rows * columns * total,
            bytes_accessed=4 * rows * columns * 4,
            transcendentals=rows * heads * total,
        ),
        name="attend",
    )(*ins)


def merged(mine, other, mine_stats):
    columns = mine.shape[1]
    heads = columns // HEAD_WIDTH

    def read(stats):
        number = 2 * heads
        stats = (
            stats[:, :number] + stats[:, number : 2 * number] + stats[:, 2 * number : 3 * number]
        )
        return stats[:, :heads], stats[:, heads:]

    top_a, sum_a = read(mine_stats)
    top_b, sum_b = read(other[:, columns:].astype(F32))
    top = jnp.maximum(top_a, top_b)
    share_a = sum_a * jnp.exp2(top_a - top)
    share_b = sum_b * jnp.exp2(top_b - top)
    total = share_a + share_b
    scale = 1.0 / jnp.maximum(total, 1e-30)
    share_a = share_a * scale
    share_b = share_b * scale
    joined = [
        mine[:, h * HEAD_WIDTH : (h + 1) * HEAD_WIDTH] * share_a[:, h : h + 1]
        + other[:, h * HEAD_WIDTH : (h + 1) * HEAD_WIDTH].astype(F32) * share_b[:, h : h + 1]
        for h in range(heads)
    ]
    return joined, top, total


def merge_kernel(mine, other, mine_stats, keep, send, stats_keep):
    blocks, count, columns = mine.shape
    half = blocks // 2
    for n in range(blocks):
        joined, top, total = merged(mine[n], other[n], mine_stats[n])
        stats = jnp.concatenate([top, total], axis=1)
        high = stats.astype(BF16).astype(F32)
        middle = (stats - high).astype(BF16).astype(F32)
        number = stats.shape[1]
        stats = jnp.concatenate(
            [
                high,
                middle,
                stats - high - middle,
                jnp.zeros((count, HEAD_WIDTH - 3 * number), F32),
            ],
            axis=1,
        )
        for h, part in enumerate(joined):
            lanes = slice(h * HEAD_WIDTH, (h + 1) * HEAD_WIDTH)
            if n < half:
                keep[n, :, lanes] = part
            else:
                send[n - half, :, lanes] = part.astype(BF16)
        if n < half:
            stats_keep[n] = stats
        else:
            send[n - half, :, columns:] = stats.astype(BF16)


def merge(mine, other, mine_stats):
    blocks, count, columns = mine.shape
    half = blocks // 2
    return pl.pallas_call(
        merge_kernel,
        out_shape=[
            jax.ShapeDtypeStruct((half, count, columns), F32),
            jax.ShapeDtypeStruct((half, count, columns + HEAD_WIDTH), BF16),
            jax.ShapeDtypeStruct((half, count, HEAD_WIDTH), F32),
        ],
        in_specs=vmem(3),
        out_specs=vmem(3),
        compiler_params=params(mine, mine, other, mine_stats),
        name="merge",
    )(mine, other, mine_stats)


def finish_kernel(chunks, *refs):
    me = lax.axis_index("wide")
    out = refs[-1]
    groups, rows, _ = out.shape
    heads = []
    for c in range(chunks):
        mine, other, stats = refs[3 * c : 3 * c + 3]
        joined, _, _ = merged(mine[0], other[0], stats[0])
        heads += joined
    whole = jnp.concatenate(heads, axis=1)
    for m in range(groups):
        out[me ^ m] = whole[m * rows : (m + 1) * rows].astype(BF16)


def finish(parts, groups):
    count = parts[0][0].shape[1]
    columns = sum(part[0].shape[2] for part in parts)
    flat = [array for part in parts for array in part]
    return pl.pallas_call(
        functools.partial(finish_kernel, len(parts)),
        out_shape=jax.ShapeDtypeStruct((groups, count // groups, columns), BF16),
        in_specs=vmem(len(flat)),
        out_specs=vmem()[0],
        compiler_params=params(*flat),
        name="finish",
    )(*flat)


def reordered(array, flip):
    if not flip:
        return array
    return jnp.stack([array[j ^ flip] for j in range(array.shape[0])])


def local(
    hidden,
    norm_gain,
    w_query,
    key_weight_matrix,
    value_weight_matrix,
    cache_key,
    prefix_value_cache,
    start,
    reach,
    passkey,
):
    blocks = lax.axis_size("blk")
    groups = lax.axis_size("wide")
    b = lax.axis_index("blk").astype(jnp.int32)
    w = lax.axis_index("wide").astype(jnp.int32)
    rows, features = hidden.shape[1:]
    count = groups * rows
    half = blocks // 2
    heads = QUERY_HEADS // groups
    columns = w_query.shape[1]
    chunks = min(CHUNKS, heads)
    kv_head = w * heads // (QUERY_HEADS // KEY_VALUE_HEADS)
    cached = cache_key.shape[0]
    cache_total = cached * blocks
    ids = jnp.stack([b, w, kv_head, jnp.int32(cache_total)])
    largest = 1.9 * 0.0625 * features * 1.01
    fit = 2.0 ** math.floor(math.log2(65504.0 / largest))

    def narrow(array):
        return (array * fit).astype(jnp.float16)

    def widen(array):
        return array.astype(F32) * (1.0 / fit)

    slices = norm(hidden, norm_gain[None, :], reach, blocks)
    sent = [swapped(slices[d], "blk", d) for d in range(1, blocks)]
    slices, cache_key, prefix_value_cache = lax.optimization_barrier(
        (slices, cache_key, prefix_value_cache)
    )
    base = kv_head * HEAD_WIDTH
    chunk = min(256, cached // 2)
    early = cached * 3 // 4 // chunk * chunk
    cache, first_rows = prepare(
        lax.dynamic_slice_in_dim(cache_key, base, HEAD_WIDTH, 1),
        lax.dynamic_slice_in_dim(prefix_value_cache, base, HEAD_WIDTH, 1),
        early,
    )
    first_rows = swapped(first_rows, "blk", 1)
    width = features // blocks
    own = jnp.stack([slices[0]] + [array[:, :width] for array in sent])
    own, first_weights, key_weight_matrix, value_weight_matrix = lax.optimization_barrier(
        (own, w_query, key_weight_matrix, value_weight_matrix)
    )

    pieces = [None] * groups
    for m in range(0, groups, 2):
        pieces[m] = swapped(own, "wide", m) if m else own
    for m in range(0, groups, 2):
        pieces[m + 1] = swapped(pieces[m], "wide", 1)

    weights = jnp.concatenate(
        [
            first_weights[:, : columns // chunks],
            lax.dynamic_slice_in_dim(key_weight_matrix, base, HEAD_WIDTH, 1),
            lax.dynamic_slice_in_dim(value_weight_matrix, base, HEAD_WIDTH, 1),
        ],
        axis=1,
    )

    shape = (blocks, count, HEAD_WIDTH)
    slot = lax.broadcasted_iota(jnp.int32, shape, 1)
    block = b ^ lax.broadcasted_iota(jnp.int32, shape, 0)
    token = ((slot // rows) ^ w) * rows + slot % rows
    cosine, sine = yarn_tables(start[0] + block * count + token, HEAD_WIDTH)
    digits = [array[:, width:] for array in sent[1::2]]
    bias = mask(ids, passkey, reach, digits, cached, groups)

    part = columns // chunks
    tokens, *first = gather(pieces, weights, part)
    projected = [first] + [
        project(tokens, w_query, blocks, c * part, part) for c in range(1, chunks)
    ]
    pair = 2 * HEAD_WIDTH
    order = list(range(chunks))
    got = {c: swapped(narrow(projected[c][1]), "blk", 1) for c in order}
    queries, sums = {}, []
    for c in order:
        keep = projected[c][0] + widen(got[c])
        sums.append(keep)
        if c == 0:
            even = keep[:, :, part : part + pair]
            odd = keep[:, :, part + pair :]
            keep = keep[:, :, :part]
        bit = half // 2
        while bit >= 1:
            out = narrow(keep)
            if c == 0:
                extra = narrow(jnp.concatenate([even[bit:], odd[bit:]], axis=0))
                even, odd = even[:bit], odd[:bit]
                if 2 * bit == half:
                    out = jnp.concatenate([out, extra], axis=2)
                    other = swapped(out, "blk", 2 * bit)
                    other, extra = other[:, :, :part], other[:, :, part:]
                else:
                    other = swapped(out, "blk", 2 * bit)
                    extra = swapped(extra, "blk", 2 * bit)
                even = even + widen(extra[:bit])
                odd = odd + widen(extra[bit:])
            else:
                other = swapped(out, "blk", 2 * bit)
            keep = keep + reordered(widen(other), bit)
            bit //= 2
        if c == 0:
            kv = jnp.concatenate([even, odd], axis=0)
        queries[c] = keep
    last_rows = swapped(rest(cache, cached - early, sums[-1:]), "blk", 1)
    parts = {}
    for c in range(chunks):
        keep, send, stats = attend(queries[c], kv, cosine, sine, bias, cache, first_rows, last_rows)
        bit = half // 2
        while bit > 1:
            keep, send, stats = merge(keep, swapped(send, "blk", 2 * bit), stats)
            bit //= 2
        parts[c] = (keep, swapped(send, "blk", 2), stats)
    parts = [parts[c] for c in range(chunks)]
    ready = finish(parts, groups)
    ready = lax.all_to_all(ready, "wide", split_axis=0, concat_axis=0, tiled=True)
    return ready.transpose(1, 0, 2).reshape(1, rows, groups * columns)


def solution(mesh):
    return jax.shard_map(
        local,
        mesh=mesh,
        in_specs=(
            P("blk", "wide", None),
            P(),
            P("blk", "wide"),
            P("blk", None),
            P("blk", None),
            P("blk", None),
            P("blk", None),
            P(),
            P("blk", None),
            P(),
        ),
        out_specs=P("blk", "wide", None),
        check_vma=False,
    )
```
